128 devices in a mesh: resp: 4 (over z_hi, core), ctx: 32 (over x, z_lo, y).
Axes of the slice: x: 4, y: 4, z: 4 (z_hi: 2, z_lo: 2; z = z_hi * 2 + z_lo), core: 2. Of those that a mesh axis runs over, the one named last changes fastest.
Arguments:
- queries: bfloat16 [4, 4096, 32, 128], P('resp', 'ctx'), may hold values from -12 to 12
- resp_keys: bfloat16 [4, 4096, 4, 128], P('resp', 'ctx'), may hold values from -6 to 6
- resp_values: bfloat16 [4, 4096, 4, 128], P('resp', 'ctx'), may hold values from -6 to 6
- prompt_keys: bfloat16 [512, 4, 128], P('ctx', 'resp'), may hold values from -6 to 6
- prompt_values: bfloat16 [512, 4, 128], P('ctx', 'resp'), may hold values from -6 to 6
- grad_out: bfloat16 [4, 4096, 32, 128], P('resp', 'ctx'), may hold values from -24 to 24
- attn_out: bfloat16 [4, 4096, 32, 128], P('resp', 'ctx'), may hold values from -6 to 6, as said below
- logsumexp: float32 [4, 4096, 32], P('resp', 'ctx'), as said below
- order: int32 [4, 4096], P('resp'), may hold values from 0 to 4095, as said below
- lengths: int32 [4], P('resp'), may hold values from 1024 to 4096, as said below
Outputs:
- grad_queries: bfloat16 [4, 4096, 32, 128], P('resp', 'ctx')
- grad_resp_keys: bfloat16 [4, 4096, 4, 128], P('resp', 'ctx')
- grad_resp_values: bfloat16 [4, 4096, 4, 128], P('resp', 'ctx')
- grad_prompt_keys: bfloat16 [512, 4, 128], P('ctx', 'resp')
- grad_prompt_values: bfloat16 [512, 4, 128], P('ctx', 'resp')
The draws below stay inside these ranges and needn't reach their ends.
Inputs may be any that keep to these rules, and one draw needn't show every extreme that they name: `order`: each row is a permutation of 0 to 4095. Cut the positions into runs of 64; the 128 slots of one index of ctx hold run a and then run 2 * 32 - 1 - a, each in rising order, with a drawn afresh for each response. `lengths`: slots whose position is at or past the length are padding; in every draw some response has all 4096 tokens live. `attn_out`: the forward output: the softmax over the visible keys (scores as in the reference program) times the values, 0 at padding slots. `logsumexp`: the log of the sum of exp(scores) over the visible keys of each live slot and head, computed in float32 by the forward pass; 0 at padding slots.
All inputs are finite; a program needn't handle non-finite values.
Results may differ from the reference program's by a relative error of at most 0.0051.
Values may be sent and summed in bfloat16 or wider, within the bound.
No kernel may reach another device: no remote copies, remote signals or barrier semaphores. Data moves between devices by JAX's collectives and lax.ppermute only.
A program may use at most 320 MiB of HBM per device.

```python
import math
import jax
import jax.numpy as jnp
from jax import lax

H = 32
KVH = 4
HD = 128
TOK_DEV = 128
GROUP = 8
LENGTH = 4096
PROMPT = 512
RESPS = 4


def mixed_normal(key, shape, spread_scale):
    first_key = jax.random.fold_in(key, 0)
    normal_part = jnp.clip(jax.random.normal(first_key, shape, jnp.float32), -6.0, 6.0)
    return spread_scale * normal_part


def raw_fields(key):
    queries = mixed_normal(jax.random.fold_in(key, 200), (RESPS, LENGTH, H, HD), 2.0)
    resp_keys = mixed_normal(jax.random.fold_in(key, 201), (RESPS, LENGTH, KVH, HD), 1.0)
    resp_values = mixed_normal(jax.random.fold_in(key, 202), (RESPS, LENGTH, KVH, HD), 1.0)
    prompt_keys = mixed_normal(jax.random.fold_in(key, 203), (PROMPT, KVH, HD), 1.0)
    prompt_values = mixed_normal(jax.random.fold_in(key, 204), (PROMPT, KVH, HD), 1.0)
    return (queries.astype(jnp.bfloat16), resp_keys.astype(jnp.bfloat16), resp_values.astype(jnp.bfloat16), prompt_keys.astype(jnp.bfloat16), prompt_values.astype(jnp.bfloat16))


def paired_positions(key):
    run_key = jax.random.fold_in(key, 301)
    devices = LENGTH // TOK_DEV
    run_len = TOK_DEV // 2
    orders = jax.vmap(lambda one_key: jax.random.permutation(one_key, devices))(jax.random.split(run_key, RESPS))
    orders = orders.astype(jnp.int32)
    offsets = jnp.arange(run_len, dtype=jnp.int32)
    first_runs = orders[:, :, None] * run_len + offsets
    second_runs = (2 * devices - 1 - orders)[:, :, None] * run_len + offsets
    return jnp.concatenate([first_runs, second_runs], axis=-1).reshape(RESPS, LENGTH).astype(jnp.int32)


def response_lengths(key):
    length_key = jax.random.fold_in(key, 302)
    first_key, second_key = jax.random.split(length_key)
    drawn = jax.random.randint(first_key, (RESPS,), LENGTH // 4, LENGTH + 1)
    full_one = jax.random.randint(second_key, (), 0, RESPS)
    return jnp.where(jnp.arange(RESPS) == full_one, LENGTH, drawn).astype(jnp.int32)


def forward_pass(fields, positions, limits):
    queries, resp_keys, resp_values, prompt_keys, prompt_values = fields
    score_scale = HD ** (-0.5)
    block_rows = math.gcd(LENGTH, 512)
    block_count = LENGTH // block_rows
    highest = lax.Precision.HIGHEST
    out_list, lse_list = ([], [])
    for member in range(RESPS):
        query_pos = positions[member]
        query_live = query_pos < limits[member]
        key_pos = jnp.concatenate([-jnp.ones((PROMPT,), jnp.int32), query_pos.astype(jnp.int32)])
        keys_all = jnp.concatenate([prompt_keys, resp_keys[member]], axis=0).astype(jnp.float32).transpose(1, 0, 2)
        values_all = jnp.concatenate([prompt_values, resp_values[member]], axis=0).astype(jnp.float32).transpose(1, 0, 2)
        query_all = queries[member].astype(jnp.float32).reshape(LENGTH, KVH, GROUP, HD).transpose(1, 0, 2, 3)

        def per_group(inputs):
            query_g, keys_g, values_g = inputs

            def per_block(block_inputs):
                query_b, pos_b, live_b = block_inputs
                scores = jnp.einsum('tgd,kd->tgk', query_b, keys_g, precision=highest) * score_scale
                visible = ((key_pos[None, :] <= pos_b[:, None]) & live_b[:, None])[:, None, :]
                masked = jnp.where(visible, scores, -1e+30)
                row_max = jnp.max(masked, axis=-1)
                weights = jnp.where(visible, jnp.exp(masked - row_max[..., None]), 0.0)
                row_total = jnp.sum(weights, axis=-1)
                safe_total = jnp.where(live_b[:, None], row_total, 1.0)
                log_total = jnp.where(live_b[:, None], row_max + jnp.log(safe_total), 0.0)
                output = jnp.einsum('tgk,kd->tgd', weights, values_g, precision=highest) / safe_total[..., None]
                output = jnp.where(live_b[:, None, None], output, 0.0)
                return (output, log_total)
            out_b, lse_b = lax.map(per_block, (query_g.reshape(block_count, block_rows, GROUP, HD), query_pos.reshape(block_count, block_rows), query_live.reshape(block_count, block_rows)))
            return (out_b.reshape(LENGTH, GROUP, HD), lse_b.reshape(LENGTH, GROUP))
        out_g, lse_g = lax.map(per_group, (query_all, keys_all, values_all))
        out_list.append(out_g.transpose(1, 0, 2, 3).reshape(LENGTH, H, HD))
        lse_list.append(lse_g.transpose(1, 0, 2).reshape(LENGTH, H))
    return (jnp.stack(out_list).astype(jnp.bfloat16), jnp.stack(lse_list))


def draw_queries(key, part):
    return raw_fields(key)[0]


def draw_resp_keys(key, part):
    return raw_fields(key)[1]


def draw_resp_values(key, part):
    return raw_fields(key)[2]


def draw_prompt_keys(key, part):
    return raw_fields(key)[3]


def draw_prompt_values(key, part):
    return raw_fields(key)[4]


def draw_attn_out(key, part):
    fields = raw_fields(key)
    return forward_pass(fields, paired_positions(key), response_lengths(key))[0]


def draw_logsumexp(key, part):
    fields = raw_fields(key)
    return forward_pass(fields, paired_positions(key), response_lengths(key))[1]


def draw_order(key, part):
    return paired_positions(key)


def draw_lengths(key, part):
    return response_lengths(key)


def shard_levels(key, dims, pieces, least, high):
    def one(dim, parts):
        draws = jax.random.uniform(jax.random.fold_in(jax.random.fold_in(key, 6), dim), (parts,), jnp.float32, least / len(pieces), high / len(pieces))
        return jnp.repeat(jnp.exp(draws), dims[dim] // parts).reshape((-1,) + (1,) * (len(dims) - dim - 1))

    gain = one(*pieces[0])
    for cut in pieces[1:]:
        gain = gain * one(*cut)
    return gain


def scatter_about(key, dims, scale, most, cuts=(), kind=jnp.bfloat16):
    entries = jax.random.normal(key, dims, jnp.float32) * scale
    if len(cuts) > 0:
        entries = shard_levels(key, dims, cuts, -0.22, 0.18) * entries
    return jnp.clip(entries, min=-most, max=most).astype(kind)


def setup_inputs(seed: int = 0) -> dict:
    splits = jax.random.split(jax.random.key(seed), 11)
    queries = draw_queries(jax.random.fold_in(splits[10], 71), 0)
    resp_keys = draw_resp_keys(jax.random.fold_in(splits[10], 71), 0)
    resp_values = draw_resp_values(jax.random.fold_in(splits[10], 71), 0)
    prompt_keys = draw_prompt_keys(jax.random.fold_in(splits[10], 71), 0)
    prompt_values = draw_prompt_values(jax.random.fold_in(splits[10], 71), 0)
    grad_out = scatter_about(splits[5], (RESPS, LENGTH, H, HD), 4.0, 24.0, ((0, 4), (1, 32)))
    attn_out = draw_attn_out(jax.random.fold_in(splits[10], 71), 0)
    logsumexp = draw_logsumexp(jax.random.fold_in(splits[10], 71), 0)
    order = draw_order(jax.random.fold_in(splits[10], 71), 0)
    lengths = draw_lengths(jax.random.fold_in(splits[10], 71), 0)
    return {"queries": queries, "resp_keys": resp_keys, "resp_values": resp_values, "prompt_keys": prompt_keys, "prompt_values": prompt_values, "grad_out": grad_out, "attn_out": attn_out, "logsumexp": logsumexp, "order": order, "lengths": lengths}


def group_grads(query_g, grad_g, lse_g, delta_g, keys_g, values_g, query_pos, query_live, key_pos):
    score_scale = HD ** -0.5
    block_rows = math.gcd(LENGTH, 512)
    block_count = LENGTH // block_rows
    keys_f = keys_g.astype(jnp.float32)
    values_f = values_g.astype(jnp.float32)
    highest = lax.Precision.HIGHEST

    def one_block(totals, inputs):
        key_total, value_total = totals
        query_b, grad_b, lse_b, delta_b, pos_b, live_b = inputs
        query_f = query_b.astype(jnp.float32)
        grad_f = grad_b.astype(jnp.float32)
        scores = jnp.einsum("tgd,kd->tgk", query_f, keys_f, precision=highest) * score_scale
        visible = (key_pos[None, :] <= pos_b[:, None]) & live_b[:, None]
        probs = jnp.where(visible[:, None, :], jnp.exp(scores - lse_b[:, :, None]), 0.0)
        dprobs = jnp.einsum("tgd,kd->tgk", grad_f, values_f, precision=highest)
        dscores = probs * (dprobs - delta_b[:, :, None])
        probs_b = lax.optimization_barrier(probs.astype(jnp.bfloat16)).astype(jnp.float32)
        dscores_b = lax.optimization_barrier(dscores.astype(jnp.bfloat16)).astype(jnp.float32)
        query_grad = jnp.einsum("tgk,kd->tgd", dscores_b, keys_f, precision=highest) * score_scale
        key_total = key_total + jnp.einsum("tgk,tgd->kd", dscores_b, query_f, precision=highest) * score_scale
        value_total = value_total + jnp.einsum("tgk,tgd->kd", probs_b, grad_f, precision=highest)
        return (key_total, value_total), query_grad

    inputs = (
        query_g.reshape(block_count, block_rows, GROUP, HD),
        grad_g.reshape(block_count, block_rows, GROUP, HD),
        lse_g.reshape(block_count, block_rows, GROUP),
        delta_g.reshape(block_count, block_rows, GROUP),
        query_pos.reshape(block_count, block_rows),
        query_live.reshape(block_count, block_rows),
    )
    zeros_kd = jnp.zeros((PROMPT + LENGTH, HD), jnp.float32)
    (key_total, value_total), query_grads = lax.scan(one_block, (zeros_kd, zeros_kd), inputs)
    return query_grads.reshape(LENGTH, GROUP, HD), key_total, value_total


def reference(queries, resp_keys, resp_values, prompt_keys, prompt_values, grad_out, attn_out, logsumexp, order, lengths):
    query_list, key_list, value_list = [], [], []
    prompt_key_sum = jnp.zeros((PROMPT, KVH, HD), jnp.float32)
    prompt_value_sum = jnp.zeros((PROMPT, KVH, HD), jnp.float32)
    for member in range(RESPS):
        query_pos = order[member].astype(jnp.int32)
        query_live = query_pos < lengths[member]
        key_pos = jnp.concatenate([-jnp.ones((PROMPT,), jnp.int32), query_pos.astype(jnp.int32)])
        keys_all = jnp.concatenate([prompt_keys, resp_keys[member]], axis=0).transpose(1, 0, 2)
        values_all = jnp.concatenate([prompt_values, resp_values[member]], axis=0).transpose(1, 0, 2)
        delta = jnp.sum(grad_out[member].astype(jnp.float32) * attn_out[member].astype(jnp.float32), axis=-1)
        query_groups = queries[member].reshape(LENGTH, KVH, GROUP, HD).transpose(1, 0, 2, 3)
        grad_groups = grad_out[member].reshape(LENGTH, KVH, GROUP, HD).transpose(1, 0, 2, 3)
        lse_groups = logsumexp[member].reshape(LENGTH, KVH, GROUP).transpose(1, 0, 2)
        delta_groups = delta.reshape(LENGTH, KVH, GROUP).transpose(1, 0, 2)

        def per_group(inputs):
            return group_grads(*inputs, query_pos, query_live, key_pos)

        query_grad, key_grad, value_grad = lax.map(
            per_group, (query_groups, grad_groups, lse_groups, delta_groups, keys_all, values_all))
        query_list.append(query_grad.transpose(1, 0, 2, 3).reshape(LENGTH, H, HD).astype(jnp.bfloat16))
        key_grad = key_grad.transpose(1, 0, 2)
        value_grad = value_grad.transpose(1, 0, 2)
        prompt_key_sum = prompt_key_sum + key_grad[:PROMPT]
        prompt_value_sum = prompt_value_sum + value_grad[:PROMPT]
        key_list.append(key_grad[PROMPT:].astype(jnp.bfloat16))
        value_list.append(value_grad[PROMPT:].astype(jnp.bfloat16))
    return (jnp.stack(query_list), jnp.stack(key_list), jnp.stack(value_list),
            prompt_key_sum.astype(jnp.bfloat16), prompt_value_sum.astype(jnp.bfloat16))
```

```python
import functools

import jax
import jax.numpy as jnp
from jax import lax
from jax.experimental import pallas as pl
from jax.experimental.pallas import tpu as pltpu
from jax.sharding import PartitionSpec as P

F32 = jnp.float32
BF16 = jnp.bfloat16
AXES = ("resp", "ctx")
LOG2E = 1.4426950408889634
RUN = 64
NT = (((1,), (1,)), ((), ()))
NN = (((1,), (0,)), ((), ()))
TN = (((0,), (0,)), ((), ()))
FAR = 1 << 20


def coords(r, c):
    return c // 8, (c // 4) % 2, c % 4, r % 2


def device_pairs(move):
    pairs = []
    for r in range(4):
        for c in range(32):
            x, z, y, _ = coords(r, c)
            r2, x2, z2, y2 = move(r, x, z, y)
            pairs.append((r * 32 + c, (r2 % 4) * 32 + (x2 % 4) * 8 + (z2 % 2) * 4 + y2 % 4))
    return pairs


def along_heads(s):
    return device_pairs(lambda r, x, z, y: (r, x, z, y + s) if r % 2 == 0 else (r, x + s, z, y))


def along_blocks(s):
    return device_pairs(lambda r, x, z, y: (r, x + s, z, y) if r % 2 == 0 else (r, x, z, y + s))


def along_z():
    return device_pairs(lambda r, x, z, y: (r, x, z + 1, y))


def along_resp(s):
    return device_pairs(lambda r, x, z, y: (r + s, x, z, y))


def send(value, pairs):
    return lax.ppermute(value, AXES, pairs)


def dot(a, b, dims):
    return lax.dot_general(a, b, dims, preferred_element_type=F32)


def grads_kernel(
    first,
    last,
    scale,
    slot_ref,
    pos_ref,
    qpos_ref,
    c0_ref,
    c1_ref,
    c2_ref,
    c3_ref,
    kv_ref,
    *rest,
):
    if first:
        dq_out, dkv_out, chunk, dkv, dq_acc = rest
        dq_in = None
    else:
        dq_in, dq_out, dkv_out, chunk, dkv, dq_acc = rest
    rows = 512
    for i, ref in enumerate((c0_ref, c1_ref, c2_ref, c3_ref)):
        chunk[pl.ds(i * 2096, 2096), :] = ref[...]
    dkv[...] = jnp.zeros_like(dkv)
    key_base = 16
    value_base = 144 + 16

    def one_run(i, _):
        base = (i // 2) * 2096
        half = i % 2
        q_rows = pl.ds(pl.multiple_of(base + half * rows, 16), rows)
        g_rows = pl.ds(pl.multiple_of(base + 1024 + half * rows, 16), rows)
        own = qpos_ref[i]
        stats = []
        for j in range(2):
            piece = chunk[pl.ds(pl.multiple_of(base + 2048, 16), 48), :].astype(F32)
            total = piece[24 * j : 24 * j + 8] + piece[24 * j + 8 : 24 * j + 16] + piece[24 * j + 16 : 24 * j + 24]
            picked = jnp.where(half == 0, total[0:4], total[4:8])
            stats.append(jnp.concatenate([picked[k : k + 1] for k in range(4)], axis=1))
        lse2, delta = stats
        acc_rows = pl.ds(pl.multiple_of(i * 128, 128), 128)
        if first:
            dq_acc[...] = jnp.zeros_like(dq_acc)
        else:
            dq_acc[...] = dq_in[acc_rows, :]

        def tile(keys, values, key_pos):
            q = chunk[q_rows, :]
            g = chunk[g_rows, :]
            s = dot(keys, q, NT)
            p = jnp.exp2(s * (scale * LOG2E) - lse2)
            if key_pos is not None:
                row_pos = own * RUN + (lax.broadcasted_iota(jnp.int32, (1, rows), 1) >> 3)
                p = jnp.where(key_pos <= row_pos, p, 0.0)
            dp = dot(values, g, NT)
            ds = (p * (dp - delta)).astype(BF16)
            dv = dot(p.astype(BF16), g, NN)
            dk = dot(ds, q, NN)
            dq_acc[...] += dot(keys, ds, TN)
            return dk, dv

        def gather(entries):
            keys = jnp.concatenate([kv_ref[pl.ds(k, n), :] for k, n, _ in entries], axis=0)
            values = jnp.concatenate([kv_ref[pl.ds(k + 144, n), :] for k, n, _ in entries], axis=0)
            return keys, values

        def scatter(entries, dk, dv):
            at = 0
            for k, n, _ in entries:
                dkv[pl.ds(k, n), :] += dk[at : at + n]
                dkv[pl.ds(k + 144, n), :] += dv[at : at + n]
                at += n

        def positions(entries):
            parts = []
            for _, n, where in entries:
                if where is None:
                    parts.append(jnp.full((n, 1), -1, jnp.int32))
                else:
                    parts.append(lax.broadcasted_iota(jnp.int32, (n, 1), 0) + where * RUN)
            return jnp.concatenate(parts, axis=0)

        def run_entry(j):
            slot = slot_ref[j]
            start = (slot // 2) * 288 + 16 + (slot % 2) * RUN
            return (pl.multiple_of(start, 16), RUN, pos_ref[j])

        def do(entries, masked):
            keys, values = gather(entries)
            dk, dv = tile(keys, values, positions(entries) if masked else None)
            scatter(entries, dk, dv)

        seen = 0
        for j in range(16):
            seen = seen + jnp.where(pos_ref[j] <= own, 1, 0)
        do([(e * 288, 16, None) for e in range(8)] + [run_entry(0), run_entry(1)], True)
        more = jnp.maximum(seen - 2, 0)
        full = jnp.maximum((more - 1) // 4, 0)

        def full_tile(t, _):
            do([run_entry(2 + 4 * t + m) for m in range(4)], False)
            return 0

        lax.fori_loop(0, full, full_tile, 0)

        @pl.when(more > 0)
        def _():
            do([run_entry(2 + 4 * full + m) for m in range(4)], True)

        if last:
            out_rows = pl.ds(pl.multiple_of(i * rows, rows), rows)
            dq_out[out_rows, :] = (dq_acc[...].T * scale).astype(BF16)
        else:
            dq_out[acc_rows, :] = dq_acc[...]
        return 0

    lax.fori_loop(0, 8, one_run, 0)
    for e in range(8):
        k_rows = pl.ds(e * 288, 144)
        v_rows = pl.ds(e * 288 + 144, 144)
        dkv_out[k_rows, :] = (dkv[k_rows, :] * scale).astype(dkv_out.dtype)
        dkv_out[v_rows, :] = dkv[v_rows, :].astype(dkv_out.dtype)


def block_grads(first, last, wide, scale, slots, poss, qpos, chunks, kv, dq):
    vmem = pl.BlockSpec(memory_space=pltpu.VMEM)
    smem = pl.BlockSpec(memory_space=pltpu.SMEM)
    operands = [slots, poss, qpos, *chunks, kv]
    specs = [smem] * 3 + [vmem] * 5
    if not first:
        operands.append(dq)
        specs.append(vmem)
    dq_shape = jax.ShapeDtypeStruct((4096, 128), BF16) if last else jax.ShapeDtypeStruct((1024, 512), F32)
    return pl.pallas_call(
        functools.partial(grads_kernel, first, last, scale),
        out_shape=[dq_shape, jax.ShapeDtypeStruct((2304, 128), F32 if wide else BF16)],
        in_specs=specs,
        out_specs=[vmem] * 2,
        scratch_shapes=[
            pltpu.VMEM((4 * 2096, 128), BF16),
            pltpu.VMEM((2304, 128), F32),
            pltpu.VMEM((128, 512), F32),
        ],
        compiler_params=pltpu.CompilerParams(vmem_limit_bytes=32 * 2**20),
        cost_estimate=pl.CostEstimate(flops=12_000_000_000, bytes_accessed=8_000_000, transcendentals=3_000_000),
    )(*operands)


def pick(stacked, index):
    return lax.dynamic_index_in_dim(stacked, index, 0, keepdims=False)


def thirds(value):
    hi = lax.reduce_precision(value, 8, 7)
    rest = value - hi
    mid = lax.reduce_precision(rest, 8, 7)
    return [hi.astype(BF16), mid.astype(BF16), (rest - mid).astype(BF16)]


def shards(
    queries,
    resp_keys,
    resp_values,
    prompt_keys,
    prompt_values,
    grad_out,
    attn_out,
    logsumexp,
    order,
    lengths,
):
    scale = queries.shape[3] ** (-0.5)
    r = lax.axis_index("resp")
    c = lax.axis_index("ctx")
    x, z, y, core = coords(r, c)
    head = jnp.where(core == 0, y, x)
    block = jnp.where(core == 0, x, y)

    prompt = jnp.stack([prompt_keys[:, 0], prompt_values[:, 0]])
    prompts = jnp.stack([prompt] + [send(prompt, along_resp(s)) for s in (1, 2, 3)])
    resp_kv = jnp.stack([resp_keys[0], resp_values[0]]).transpose(2, 0, 1, 3)

    def kv_chunk(g):
        rows = jnp.concatenate([pick(prompts, (r - g) % 4), pick(resp_kv, g)], axis=1)
        return rows.reshape(288, 128)

    pieces = [kv_chunk(head)]
    for s in (1, 2, 3):
        pieces.append(send(kv_chunk((head + s) % 4), along_heads(s)))
    near = jnp.concatenate(pieces, axis=0)
    kv_own = jnp.concatenate([near, send(near, along_z())], axis=0)
    kv_blocks = {0: kv_own}
    for s in (1, 3, 2):
        kv_blocks[s] = send(kv_own, along_blocks(s))

    query_pos = lax.dynamic_slice_in_dim(order[0], c * 128, 128)
    live = query_pos < lengths[0]
    delta = jnp.sum(grad_out[0].astype(F32) * attn_out[0].astype(F32), axis=-1)
    lse2 = jnp.where(live[:, None], logsumexp[0] * LOG2E, 1e30)
    stats = jnp.stack([lse2, delta]).reshape(2, 128, 4, 8).transpose(2, 0, 1, 3).reshape(4, 2, 8, 128)
    stats = jnp.stack(thirds(stats), axis=2).reshape(4, 48, 128)
    q_four = queries[0].reshape(128, 4, 8, 128)
    g_four = grad_out[0].reshape(128, 4, 8, 128)

    def q_chunk(g):
        q = lax.dynamic_index_in_dim(q_four, g, 1, keepdims=False).reshape(1024, 128)
        do = lax.dynamic_index_in_dim(g_four, g, 1, keepdims=False).reshape(1024, 128)
        return jnp.concatenate([q, do, pick(stats, g)], axis=0)

    chunks = [q_chunk(head)]
    for s in (1, 2, 3):
        chunks.append(send(q_chunk((head + s) % 4), along_heads(s)))

    run_pos = order[0].reshape(32, 2, RUN)[:, :, 0] // RUN
    shift_b = lax.broadcasted_iota(jnp.int32, (4, 2, 4, 1), 0)
    shift_z = lax.broadcasted_iota(jnp.int32, (4, 2, 4, 1), 1)
    shift_h = lax.broadcasted_iota(jnp.int32, (4, 2, 4, 1), 2)
    from_b = (block - shift_b) % 4
    from_h = (head - shift_h) % 4
    from_z = (z + shift_z) % 2
    owner = jnp.where(core == 0, from_b * 8 + from_h, from_h * 8 + from_b) + from_z * 4
    hit = owner[..., None] == jnp.arange(32, dtype=jnp.int32).reshape(1, 1, 1, 1, 32)
    runs = jnp.sum(jnp.where(hit, run_pos.T.reshape(1, 1, 1, 2, 32), 0), axis=-1)
    qpos = runs[0, 0].reshape(8)
    runs = runs.reshape(4, 16)
    rank = jnp.sum((runs[:, None, :] < runs[:, :, None]).astype(jnp.int32), axis=-1)
    place = rank[:, None, :] == jnp.arange(16, dtype=jnp.int32)[None, :, None]
    slots = jnp.sum(jnp.where(place, jnp.arange(16, dtype=jnp.int32)[None, None, :], 0), axis=-1)
    poss = jnp.sum(jnp.where(place, runs[:, None, :], 0), axis=-1)
    slots = jnp.pad(slots, ((0, 0), (0, 4)))
    poss = jnp.pad(poss, ((0, 0), (0, 4)), constant_values=FAR)

    dq = None
    totals = None
    turns = (0, 1, 3, 2)
    for i, s in enumerate(turns):
        dq, dkv = block_grads(
            i == 0, i == 3, s == 0, scale, slots[s], poss[s], qpos, chunks, kv_blocks[s], dq
        )
        if s == 0:
            totals = dkv
        else:
            totals = totals + send(dkv, along_blocks(4 - s)).astype(F32)

    back = [dq[:1024]]
    for s in (1, 2, 3):
        back.append(send(dq[1024 * s : 1024 * (s + 1)], along_heads(4 - s)))
    back = jnp.stack(back).reshape(4, 128, 8, 128)
    turn = (4 - head) % 4
    grad_queries = lax.dynamic_slice_in_dim(jnp.concatenate([back, back[:3]], axis=0), turn, 4, 0)
    grad_queries = grad_queries.transpose(1, 0, 2, 3).reshape(1, 128, 32, 128)

    mine = totals[:1152] + send(totals[1152:].astype(BF16), along_z()).astype(F32)
    mine = mine.astype(BF16).reshape(4, 2, 144, 128)
    rows = [mine[0]]
    for s in (1, 2, 3):
        rows.append(send(mine[s], along_heads(4 - s)))
    rows = jnp.stack(rows)
    rows = lax.dynamic_slice_in_dim(jnp.concatenate([rows, rows[:3]], axis=0), turn, 4, 0)
    grad_resp = rows[:, :, 16:].transpose(1, 2, 0, 3)
    parts = rows[:, :, :16]
    prompt_sum = pick(parts, r).astype(F32)
    for s in (1, 2, 3):
        prompt_sum = prompt_sum + send(pick(parts, (r + s) % 4), along_resp(s)).astype(F32)
    prompt_sum = prompt_sum.astype(BF16)
    return (
        grad_queries,
        grad_resp[0][None],
        grad_resp[1][None],
        prompt_sum[0][:, None],
        prompt_sum[1][:, None],
    )


def solution(mesh):
    wide = P("resp", "ctx", None, None)
    prompt = P("ctx", "resp", None)
    return jax.shard_map(
        shards,
        mesh=mesh,
        in_specs=(
            wide,
            wide,
            wide,
            prompt,
            prompt,
            wide,
            wide,
            P("resp", "ctx", None),
            P("resp", None),
            P("resp"),
        ),
        out_specs=(wide, wide, wide, prompt, prompt),
        check_vma=False,
    )
```

```python
import functools

import jax
import jax.numpy as jnp
from jax import lax
from jax.experimental import pallas as pl
from jax.experimental.pallas import tpu as pltpu
from jax.sharding import PartitionSpec as P

F32 = jnp.float32
BF16 = jnp.bfloat16
AXES = ("resp", "ctx")
LOG2E = 1.4426950408889634
RUN = 64
NT = (((1,), (1,)), ((), ()))
NN = (((1,), (0,)), ((), ()))
TN = (((0,), (0,)), ((), ()))


def coords(r, c):
    return c // 8, (c // 4) % 2, c % 4, r % 2


def device_pairs(move):
    pairs = []
    for r in range(4):
        for c in range(32):
            x, z, y, _ = coords(r, c)
            r2, x2, z2, y2 = move(r, x, z, y)
            pairs.append((r * 32 + c, (r2 % 4) * 32 + (x2 % 4) * 8 + (z2 % 2) * 4 + y2 % 4))
    return pairs


def along_heads(s):
    return device_pairs(lambda r, x, z, y: (r, x, z, y + s) if r % 2 == 0 else (r, x + s, z, y))


def along_blocks(s):
    return device_pairs(lambda r, x, z, y: (r, x + s, z, y) if r % 2 == 0 else (r, x, z, y + s))


def along_z():
    return device_pairs(lambda r, x, z, y: (r, x, z + 1, y))


def along_both(s):
    return device_pairs(lambda r, x, z, y: (r, x + s, z + 1, y) if r % 2 == 0 else (r, x, z + 1, y + s))


def along_resp(s):
    return device_pairs(lambda r, x, z, y: (r + s, x, z, y))


def across_cores():
    return device_pairs(lambda r, x, z, y: (r ^ 1, x, z, y))


def across_z_hi():
    return device_pairs(lambda r, x, z, y: (r ^ 2, x, z, y))


def send(value, pairs):
    return lax.ppermute(value, AXES, pairs)


def dot(a, b, dims):
    return lax.dot_general(a, b, dims, preferred_element_type=F32)


def grads_kernel(shift, members, first, last, scale, received, at_ref, stats_ref, c0_ref, c1_ref, c2_ref, c3_ref, *rest):
    parts = members // 4
    rest = list(rest)
    kv_refs = [rest.pop(0) for _ in range(parts)]
    dq_in = None if first else rest.pop(0)
    held = [rest.pop(0) for _ in range(received)]
    dq_out = rest.pop(0)
    outs = [rest.pop(0) for _ in range(parts)]
    chunk, keys, values, dkeys, dvalues, stage, meta_ref = rest[:7]
    dq = rest[7] if last else dq_out
    core, head, block, z = [at_ref[64 + i] for i in range(4)]

    def runs_of(from_b, from_h, from_z):
        c = jnp.where(core == 0, from_b * 8 + from_h, from_h * 8 + from_b) + from_z * 4
        one, two = at_ref[2 * c], at_ref[2 * c + 1]
        return jnp.minimum(one, two), jnp.where(one > two, 1, 0)

    if members == 8:
        places_in = [(zz * 1152, zz, e) for zz in range(2) for e in range(4)]
    else:
        places_in = [(0, 0 if last else 1, e) for e in range(4)]
    found = [runs_of((block - shift) & 3, (head - e) & 3, (z + zz) & 1) for _, zz, e in places_in]
    for j, (early_j, swap_j) in enumerate(found):
        rank = 0
        for i, (early_i, _) in enumerate(found):
            if i != j:
                rank = rank + jnp.where(early_i < early_j, 1, 0)
        start = places_in[j][0] + 288 * places_in[j][2]
        meta_ref[rank] = early_j
        meta_ref[8 + rank] = start + RUN * swap_j
        meta_ref[16 + rank] = start + RUN * (1 - swap_j)
    for e in range(4):
        meta_ref[24 + e], meta_ref[28 + e] = runs_of(block, (head - e) & 3, z)
    rows = 512
    prompt = 16 * members
    for i, ref in enumerate((c0_ref, c1_ref, c2_ref, c3_ref)):
        chunk[pl.ds(i * 2048, 2048), :] = ref[...]
    if first:
        dq[...] = jnp.zeros_like(dq)
    else:
        dq[...] = dq_in[...]
    dkeys[...] = jnp.zeros_like(dkeys)
    dvalues[...] = jnp.zeros_like(dvalues)

    def places(u):
        for late in range(2):
            at = meta_ref[8 + 8 * late + u]
            yield at, pl.ds(prompt + (late * members + u) * RUN, RUN)

    for part in range(parts):
        stage[pl.ds(part * 1152, 1152), :] = kv_refs[part][...]
    for e in range(members):
        to = pl.ds(16 * e, 16)
        keys[to, :] = stage[pl.ds(288 * e + 256, 16), :]
        values[to, :] = stage[pl.ds(288 * e + 272, 16), :]
    for u in range(members):
        for at, to in places(u):
            keys[to, :] = stage[pl.ds(pl.multiple_of(at, 16), RUN), :]
            values[to, :] = stage[pl.ds(pl.multiple_of(at + 128, 16), RUN), :]

    slope = lax.broadcasted_iota(jnp.int32, (RUN, rows), 0) - (
        lax.broadcasted_iota(jnp.int32, (RUN, rows), 1) >> 3
    )

    def one_chunk(i, _):
        base = i * 2048
        early = meta_ref[24 + i]
        early_half = meta_ref[28 + i]
        piece = stats_ref[pl.ds(pl.multiple_of(i * 48, 16), 48), :].astype(F32)

        def tile(half, key_row, count, marks):
            q_rows = pl.ds(pl.multiple_of(base + half * rows, 16), rows)
            g_rows = pl.ds(pl.multiple_of(base + 1024 + half * rows, 16), rows)
            stats = []
            for j in range(2):
                total = piece[24 * j : 24 * j + 8] + piece[24 * j + 8 : 24 * j + 16] + piece[24 * j + 16 : 24 * j + 24]
                picked = jnp.where(half == 0, total[0:4], total[4:8])
                stats.append(jnp.concatenate([picked[k : k + 1] for k in range(4)], axis=1))
            lse2, delta = stats
            k_rows = pl.ds(key_row, count)
            kt = keys[k_rows, :]
            q = chunk[q_rows, :]
            g = chunk[g_rows, :]
            p = jnp.exp2(dot(kt, q, NT) * (scale * LOG2E) - lse2)
            if marks:
                cut = [p[: marks[0][0]]] if marks[0][0] else []
                for at, limit in marks:
                    cut.append(jnp.where(slope <= limit, p[at : at + RUN], 0.0))
                p = jnp.concatenate(cut, axis=0)
            ds = (p * (dot(values[k_rows, :], g, NT) - delta)).astype(BF16)
            dvalues[k_rows, :] += dot(p.astype(BF16), g, NN)
            dkeys[k_rows, :] += dot(ds, q, NN)
            acc = pl.ds(pl.multiple_of((2 * i + half) * 128, 128), 128)
            dq[acc, :] += dot(kt, ds, TN)

        def early_limit(u):
            return (early - meta_ref[u]) * RUN

        def late_limit(u):
            return (meta_ref[u] - early) * RUN

        late_half = 1 - early_half
        late_row = prompt + members * RUN
        tile(late_half, 0, late_row, [])
        tile(early_half, 0, prompt + 256, [(prompt + RUN * u, early_limit(u)) for u in range(4)])
        if members == 8:
            seen = 0
            for u in range(8):
                seen = seen + jnp.where(meta_ref[u] <= early, 1, 0)
            more = seen > 4
            tile(
                jnp.where(more, early_half, late_half),
                pl.multiple_of(jnp.where(more, prompt + 256, late_row), 16),
                256,
                [(RUN * u, jnp.where(more, early_limit(4 + u), late_limit(u))) for u in range(4)],
            )
        top = members - 4
        tile(late_half, late_row + RUN * top, 256, [(RUN * u, late_limit(top + u)) for u in range(4)])
        return 0

    lax.fori_loop(0, 4, one_chunk, 0)

    if last:
        for i in range(8):
            dq_out[pl.ds(i * rows, rows), :] = (dq[pl.ds(i * 128, 128), :].T * scale).astype(BF16)

    wide = outs[0].dtype
    total = outs[0] if last else stage
    for e in range(members):
        at = pl.ds(16 * e, 16)
        total[pl.ds(288 * e + 256, 16), :] = (dkeys[at, :] * scale).astype(wide)
        total[pl.ds(288 * e + 272, 16), :] = dvalues[at, :].astype(wide)
    for u in range(members):
        for at, frm in places(u):
            total[pl.ds(pl.multiple_of(at, 16), RUN), :] = (dkeys[frm, :] * scale).astype(wide)
            total[pl.ds(pl.multiple_of(at + 128, 16), RUN), :] = dvalues[frm, :].astype(wide)
    if not last:
        for part in range(parts):
            outs[part][...] = stage[pl.ds(part * 1152, 1152), :]
    for ref in held if last else []:
        outs[0][...] += ref[...].astype(F32)


def block_grads(shift, first, last, scale, at, stats, chunks, kv, dq, held):
    parts = len(kv)
    members = 4 * parts
    vmem = pl.BlockSpec(memory_space=pltpu.VMEM)
    smem = pl.BlockSpec(memory_space=pltpu.SMEM)
    operands = [at, stats, *chunks, *kv] + ([] if first else [dq]) + list(held)
    specs = [smem] + [vmem] * (5 + parts + (0 if first else 1))
    specs += [vmem if last else pl.BlockSpec(memory_space=pl.ANY)] * len(held)
    dq_shape = jax.ShapeDtypeStruct((4096, 128), BF16) if last else jax.ShapeDtypeStruct((1024, 512), F32)
    sorted_rows = 144 * members
    scratch = [
        pltpu.VMEM((4 * 2048, 128), BF16),
        pltpu.VMEM((sorted_rows, 128), BF16),
        pltpu.VMEM((sorted_rows, 128), BF16),
        pltpu.VMEM((sorted_rows, 128), F32),
        pltpu.VMEM((sorted_rows, 128), F32),
        pltpu.VMEM((1152 * parts, 128), BF16),
        pltpu.SMEM((32,), jnp.int32),
    ]
    if last:
        scratch.append(pltpu.VMEM((1024, 512), F32))
    return pl.pallas_call(
        functools.partial(grads_kernel, shift, members, first, last, scale, len(held)),
        out_shape=[dq_shape] + [jax.ShapeDtypeStruct((1152, 128), F32 if last else BF16)] * parts,
        in_specs=specs,
        out_specs=[vmem] * (1 + parts),
        scratch_shapes=scratch,
        compiler_params=pltpu.CompilerParams(vmem_limit_bytes=32 * 2**20),
        cost_estimate=pl.CostEstimate(
            flops=5_000_000_000 * parts, bytes_accessed=8_000_000, transcendentals=1_500_000 * parts
        ),
    )(*operands)


def chunks_kernel(at_ref, x_ref, kv_ref, p0_ref, p1_ref, p2_ref, p3_ref, o0_ref, o1_ref, o2_ref, o3_ref, prompts):
    head, r = at_ref[65], at_ref[68]
    for i, ref in enumerate((p0_ref, p1_ref, p2_ref, p3_ref)):
        prompts[i] = ref[...]
    terms = []
    for j in range(2):
        rest = x_ref[j]
        for _ in range(3):
            term = rest.astype(BF16)
            terms.append(term)
            rest = rest - term.astype(F32)
    terms = jnp.concatenate(terms, axis=0)
    slot = lax.broadcasted_iota(jnp.int32, (768, 128), 0)
    lane = lax.broadcasted_iota(jnp.int32, (768, 128), 1)
    here = (slot & 15) == (lane >> 3)
    to_row = lax.broadcasted_iota(jnp.int32, (48, 768), 0)
    from_slot = lax.broadcasted_iota(jnp.int32, (48, 768), 1)
    gather = (to_row == (from_slot >> 4)).astype(BF16)
    from_head = lax.broadcasted_iota(jnp.int32, (32, 128), 0)
    to_head = lax.broadcasted_iota(jnp.int32, (32, 128), 1) & 7
    for s, ref in enumerate((o0_ref, o1_ref, o2_ref, o3_ref)):
        g = (head + s) & 3
        spread = dot(terms, (from_head == to_head + 8 * g).astype(BF16), NN)
        ref[pl.ds(0, 256), :] = kv_ref[g]
        ref[pl.ds(256, 32), :] = prompts[(r - g) & 3]
        ref[pl.ds(288, 48), :] = dot(gather, jnp.where(here, spread, 0.0).astype(BF16), NN).astype(BF16)


def pick(stacked, index):
    return lax.dynamic_index_in_dim(stacked, index, 0, keepdims=False)


def make_chunks(at, x, kv, prompts):
    vmem = pl.BlockSpec(memory_space=pltpu.VMEM)
    return pl.pallas_call(
        chunks_kernel,
        out_shape=[jax.ShapeDtypeStruct((336, 128), BF16)] * 4,
        in_specs=[pl.BlockSpec(memory_space=pltpu.SMEM)] + [vmem] * 6,
        out_specs=[vmem] * 4,
        scratch_shapes=[pltpu.VMEM((4, 32, 128), BF16)],
        compiler_params=pltpu.CompilerParams(vmem_limit_bytes=16 * 2**20),
        cost_estimate=pl.CostEstimate(flops=200_000_000, bytes_accessed=1_000_000, transcendentals=0),
    )(at, x, kv, *prompts)


def shards(
    queries,
    resp_keys,
    resp_values,
    prompt_keys,
    prompt_values,
    grad_out,
    attn_out,
    logsumexp,
    order,
    lengths,
):
    scale = queries.shape[3] ** (-0.5)
    r = lax.axis_index("resp")
    c = lax.axis_index("ctx")
    x, z, y, core = coords(r, c)
    head = jnp.where(core == 0, y, x)
    block = jnp.where(core == 0, x, y)

    q_four = queries[0].reshape(128, 4, 8, 128)
    g_four = grad_out[0].reshape(128, 4, 8, 128)

    def q_chunk(g):
        q = lax.dynamic_index_in_dim(q_four, g, 1, keepdims=False).reshape(1024, 128)
        do = lax.dynamic_index_in_dim(g_four, g, 1, keepdims=False).reshape(1024, 128)
        return jnp.concatenate([q, do], axis=0)

    chunks = [q_chunk(head)] + [send(q_chunk((head + s) % 4), along_heads(s)) for s in (1, 3)]
    far_chunk = q_chunk((head + 2) % 4)

    prompt = jnp.concatenate([prompt_keys[:, 0], prompt_values[:, 0]], axis=0)
    prompts = [prompt] + [send(prompt, along_resp(s)) for s in (1, 2, 3)]
    query_pos = lax.dynamic_slice_in_dim(order[0], c * 128, 128)
    live = query_pos < lengths[0]
    delta = jnp.sum(grad_out[0].astype(F32) * attn_out[0].astype(F32), axis=-1)
    x_stats = jnp.stack([jnp.where(live[:, None], logsumexp[0] * LOG2E, 1e30), delta])
    resp_kv = jnp.stack([resp_keys[0], resp_values[0]]).transpose(2, 0, 1, 3).reshape(4, 256, 128)
    run_pos = order[0].reshape(64, RUN)[:, 0] // RUN
    at = jnp.concatenate([run_pos, jnp.stack([core, head, block, z, r])])
    pieces = make_chunks(at, x_stats, resp_kv, prompts)
    pieces = [pieces[0]] + [send(pieces[s], along_heads(s)) for s in (1, 2, 3)]
    near = jnp.concatenate([piece[:288] for piece in pieces], axis=0)
    stats = jnp.concatenate([piece[288:] for piece in pieces], axis=0)
    near, far_chunk, *chunks = lax.optimization_barrier((near, far_chunk, *chunks))
    chunks = [chunks[0], chunks[1], send(far_chunk, along_heads(2)), chunks[2]]
    far = send(near, along_z())
    own = jnp.concatenate([near, far], axis=0)
    kv_blocks = {s: send(own, along_blocks(s)) for s in (1, 3, 2)}

    dq, sent = block_grads(0, True, False, scale, at, stats, chunks, [far], None, [])
    got = {0: [send(sent, along_z())]}
    for i, s in enumerate((1, 3, 2)):
        held = got[0] if i == 1 else got[1] if i == 2 else []
        half = kv_blocks[s]
        dq, near_part, far_part = block_grads(
            s, False, False, scale, at, stats, chunks, [half[:1152], half[1152:]], dq, held
        )
        got[s] = [send(near_part, along_blocks(4 - s)), send(far_part, along_both(4 - s))]
    dq, totals = block_grads(0, False, True, scale, at, stats, chunks, [near], dq, got[0] + got[1] + got[3])

    dq, *late = lax.optimization_barrier((dq, *got[2]))
    back = [dq[:1024]]
    for s in (1, 2, 3):
        back.append(send(dq[1024 * s : 1024 * (s + 1)], along_heads(4 - s)))
    back = jnp.stack(back).reshape(4, 128, 8, 128)
    turn = (4 - head) % 4
    grad_queries = lax.dynamic_slice_in_dim(jnp.concatenate([back, back[:3]], axis=0), turn, 4, 0)
    grad_queries = grad_queries.transpose(1, 0, 2, 3).reshape(1, 128, 32, 128)

    for part in late:
        totals = totals + part.astype(F32)
    mine = totals.astype(BF16).reshape(4, 288, 128)
    rows = [mine[0]]
    for s in (1, 2, 3):
        rows.append(send(mine[s], along_heads(4 - s)))
    rows = jnp.stack(rows)
    rows = lax.dynamic_slice_in_dim(jnp.concatenate([rows, rows[:3]], axis=0), turn, 4, 0)
    grad_resp = rows[:, :256].reshape(4, 2, 128, 128).transpose(1, 2, 0, 3)
    parts = rows[:, 256:]
    mine_pair = pick(parts.reshape(2, 2, 32, 128).transpose(1, 0, 2, 3), core).astype(F32)
    theirs = pick(parts.reshape(2, 2, 32, 128).transpose(1, 0, 2, 3), 1 - core)
    mine_pair = mine_pair + send(theirs, across_cores()).astype(F32)
    prompt_sum = pick(mine_pair, r // 2) + send(pick(mine_pair, 1 - r // 2), across_z_hi())
    prompt_sum = prompt_sum.astype(BF16).reshape(2, 16, 128)
    return (
        grad_queries,
        grad_resp[0][None],
        grad_resp[1][None],
        prompt_sum[0][:, None],
        prompt_sum[1][:, None],
    )


def solution(mesh):
    wide = P("resp", "ctx", None, None)
    prompt = P("ctx", "resp", None)
    return jax.shard_map(
        shards,
        mesh=mesh,
        in_specs=(
            wide,
            wide,
            wide,
            prompt,
            prompt,
            wide,
            wide,
            P("resp", "ctx", None),
            P("resp", None),
            P("resp"),
        ),
        out_specs=(wide, wide, wide, prompt, prompt),
        check_vma=False,
    )
```

```python
import functools

import jax
import jax.numpy as jnp
from jax import lax
from jax.experimental import pallas as pl
from jax.experimental.pallas import tpu as pltpu
from jax.sharding import PartitionSpec as P

F32 = jnp.float32
BF16 = jnp.bfloat16
AXES = ("resp", "ctx")
LOG2E = 1.4426950408889634
RUN = 64
NT = (((1,), (1,)), ((), ()))
NN = (((1,), (0,)), ((), ()))
TN = (((0,), (0,)), ((), ()))


def coords(r, c):
    return c // 8, (c // 4) % 2, c % 4, r % 2


def device_pairs(move):
    pairs = []
    for r in range(4):
        for c in range(32):
            x, z, y, _ = coords(r, c)
            r2, x2, z2, y2 = move(r, x, z, y)
            pairs.append((r * 32 + c, (r2 % 4) * 32 + (x2 % 4) * 8 + (z2 % 2) * 4 + y2 % 4))
    return pairs


def along_heads(s):
    return device_pairs(lambda r, x, z, y: (r, x, z, y + s) if r % 2 == 0 else (r, x + s, z, y))


def along_blocks(s):
    return device_pairs(lambda r, x, z, y: (r, x + s, z, y) if r % 2 == 0 else (r, x, z, y + s))


def along_z():
    return device_pairs(lambda r, x, z, y: (r, x, z + 1, y))


def along_both(s):
    return device_pairs(lambda r, x, z, y: (r, x + s, z + 1, y) if r % 2 == 0 else (r, x, z + 1, y + s))


def along_resp(s):
    return device_pairs(lambda r, x, z, y: (r + s, x, z, y))


def across_cores():
    return device_pairs(lambda r, x, z, y: (r ^ 1, x, z, y))


def across_z_hi():
    return device_pairs(lambda r, x, z, y: (r ^ 2, x, z, y))


def send(value, pairs):
    return lax.ppermute(value, AXES, pairs)


def dot(a, b, dims):
    return lax.dot_general(a, b, dims, preferred_element_type=F32)


def grads_kernel(halves, blocks, first, last, scale, received, at_ref, stats_ref, c0_ref, c1_ref, c2_ref, c3_ref, *rest):
    parts = len(halves)
    members = 4 * parts
    rest = list(rest)
    kv_refs = [rest.pop(0) for _ in range(blocks)]
    dq_in = None if first else rest.pop(0)
    held = [rest.pop(0) for _ in range(received)]
    dq_outs = [rest.pop(0) for _ in range(4 if last else 1)]
    outs = [rest.pop(0) for _ in range(parts)]
    chunk, keys, values, dkeys, dvalues, stage, meta_ref = rest[:7]
    dq = rest[7] if last else dq_outs[0]
    core, head, block, z = [at_ref[64 + i] for i in range(4)]

    def runs_of(from_b, from_h, from_z):
        c = jnp.where(core == 0, from_b * 8 + from_h, from_h * 8 + from_b) + from_z * 4
        one, two = at_ref[2 * c], at_ref[2 * c + 1]
        return jnp.minimum(one, two), jnp.where(one > two, 1, 0)

    places_in = [(part, e) for part in range(parts) for e in range(4)]
    found = [
        runs_of((block - halves[part][0]) & 3, (head - e) & 3, (z + halves[part][1]) & 1) for part, e in places_in
    ]
    for j, (early_j, swap_j) in enumerate(found):
        rank = 0
        for i, (early_i, _) in enumerate(found):
            if i != j:
                rank = rank + jnp.where(early_i < early_j, 1, 0)
        start = 1152 * places_in[j][0] + 288 * places_in[j][1]
        meta_ref[rank] = early_j
        meta_ref[16 + rank] = start + RUN * swap_j
        meta_ref[32 + rank] = start + RUN * (1 - swap_j)
    for e in range(4):
        meta_ref[48 + e], meta_ref[52 + e] = runs_of(block, (head - e) & 3, z)
    rows = 512
    prompt = 16 * members
    for i, ref in enumerate((c0_ref, c1_ref, c2_ref, c3_ref)):
        chunk[pl.ds(i * 2048, 2048), :] = ref[...]
    if first:
        dq[...] = jnp.zeros_like(dq)
    else:
        dq[...] = dq_in[...]
    dkeys[...] = jnp.zeros_like(dkeys)
    dvalues[...] = jnp.zeros_like(dvalues)

    def places(u):
        for late in range(2):
            at = meta_ref[16 + 16 * late + u]
            yield at, pl.ds(prompt + (late * members + u) * RUN, RUN)

    at = 0
    for ref in kv_refs:
        stage[pl.ds(at, ref.shape[0]), :] = ref[...]
        at += ref.shape[0]
    for e in range(members):
        to = pl.ds(16 * e, 16)
        keys[to, :] = stage[pl.ds(288 * e + 256, 16), :]
        values[to, :] = stage[pl.ds(288 * e + 272, 16), :]
    for u in range(members):
        for at, to in places(u):
            keys[to, :] = stage[pl.ds(pl.multiple_of(at, 16), RUN), :]
            values[to, :] = stage[pl.ds(pl.multiple_of(at + 128, 16), RUN), :]

    slope = lax.broadcasted_iota(jnp.int32, (RUN, rows), 0) - (
        lax.broadcasted_iota(jnp.int32, (RUN, rows), 1) >> 3
    )

    def one_chunk(i, _):
        base = i * 2048
        early = meta_ref[48 + i]
        early_half = meta_ref[52 + i]
        piece = stats_ref[pl.ds(pl.multiple_of(i * 48, 16), 48), :].astype(F32)

        def tile(half, spans, marks):
            q_rows = pl.ds(pl.multiple_of(base + half * rows, 16), rows)
            g_rows = pl.ds(pl.multiple_of(base + 1024 + half * rows, 16), rows)
            stats = []
            for j in range(2):
                total = piece[24 * j : 24 * j + 8] + piece[24 * j + 8 : 24 * j + 16] + piece[24 * j + 16 : 24 * j + 24]
                picked = jnp.where(half == 0, total[0:4], total[4:8])
                stats.append(jnp.concatenate([picked[k : k + 1] for k in range(4)], axis=1))
            lse2, delta = stats
            spans = [pl.ds(at, count) for at, count in spans]
            kt = jnp.concatenate([keys[span, :] for span in spans], axis=0)
            vt = jnp.concatenate([values[span, :] for span in spans], axis=0)
            q = chunk[q_rows, :]
            g = chunk[g_rows, :]
            s = dot(kt, q, NT)
            dp = dot(vt, g, NT)
            p = jnp.exp2(s * (scale * LOG2E) - lse2)
            if marks:
                cut = [p[: marks[0][0]]] if marks[0][0] else []
                for at, limit in marks:
                    cut.append(jnp.where(slope <= limit, p[at : at + RUN], 0.0))
                p = jnp.concatenate(cut, axis=0)
            ds = (p * (dp - delta)).astype(BF16)
            dv = dot(p.astype(BF16), g, NN)
            dk = dot(ds, q, NN)
            at = 0
            for span in spans:
                dvalues[span, :] += dv[at : at + span.size]
                dkeys[span, :] += dk[at : at + span.size]
                at += span.size
            acc = pl.ds(pl.multiple_of((2 * i + half) * 128, 128), 128)
            dq[acc, :] += dot(kt, ds, TN)

        def early_limit(u):
            return (early - meta_ref[u]) * RUN

        def late_limit(u):
            return (meta_ref[u] - early) * RUN

        late_half = 1 - early_half
        late_row = prompt + members * RUN
        top = members - 4
        tile(
            late_half,
            [(0, late_row), (late_row + RUN * top, 256)],
            [(late_row + RUN * u, late_limit(top + u)) for u in range(4)],
        )
        tile(early_half, [(0, prompt + 256)], [(prompt + RUN * u, early_limit(u)) for u in range(4)])
        seen = 0
        for u in range(members):
            seen = seen + jnp.where(meta_ref[u] <= early, 1, 0)
        for i_tile in range(1, parts):
            more = seen > 4 * i_tile
            low, high = 4 * i_tile, 4 * (i_tile - 1)
            tile(
                jnp.where(more, early_half, late_half),
                [(pl.multiple_of(jnp.where(more, prompt + RUN * low, late_row + RUN * high), 16), 256)],
                [(RUN * u, jnp.where(more, early_limit(low + u), late_limit(high + u))) for u in range(4)],
            )
        return 0

    lax.fori_loop(0, 4, one_chunk, 0, unroll=(4, 2, 1, 1)[parts - 1])

    if last:
        for i in range(8):
            dq_outs[i // 2][pl.ds(i % 2 * rows, rows), :] = (dq[pl.ds(i * 128, 128), :].T * scale).astype(BF16)

    wide = outs[0].dtype
    total = outs[0] if last else stage
    for e in range(members):
        at = pl.ds(16 * e, 16)
        total[pl.ds(288 * e + 256, 16), :] = (dkeys[at, :] * scale).astype(wide)
        total[pl.ds(288 * e + 272, 16), :] = dvalues[at, :].astype(wide)
    for u in range(members):
        for at, frm in places(u):
            total[pl.ds(pl.multiple_of(at, 16), RUN), :] = (dkeys[frm, :] * scale).astype(wide)
            total[pl.ds(pl.multiple_of(at + 128, 16), RUN), :] = dvalues[frm, :].astype(wide)
    if not last:
        for part in range(parts):
            outs[part][...] = stage[pl.ds(part * 1152, 1152), :]
    for ref in held if last else []:
        outs[0][...] += ref[...].astype(F32)


def block_grads(halves, first, last, scale, at, stats, chunks, kv, dq, held):
    parts = len(halves)
    members = 4 * parts
    vmem = pl.BlockSpec(memory_space=pltpu.VMEM)
    smem = pl.BlockSpec(memory_space=pltpu.SMEM)
    operands = [at, stats, *chunks, *kv] + ([] if first else [dq]) + list(held)
    specs = [smem] + [vmem] * (5 + len(kv) + (0 if first else 1))
    specs += [vmem if last else pl.BlockSpec(memory_space=pl.ANY)] * len(held)
    dq_shapes = [jax.ShapeDtypeStruct((1024, 128), BF16)] * 4 if last else [jax.ShapeDtypeStruct((1024, 512), F32)]
    sorted_rows = 144 * members
    scratch = [
        pltpu.VMEM((4 * 2048, 128), BF16),
        pltpu.VMEM((sorted_rows, 128), BF16),
        pltpu.VMEM((sorted_rows, 128), BF16),
        pltpu.VMEM((sorted_rows, 128), F32),
        pltpu.VMEM((sorted_rows, 128), F32),
        pltpu.VMEM((1152 * parts, 128), BF16),
        pltpu.SMEM((64,), jnp.int32),
    ]
    if last:
        scratch.append(pltpu.VMEM((1024, 512), F32))
    return pl.pallas_call(
        functools.partial(grads_kernel, halves, len(kv), first, last, scale, len(held)),
        out_shape=dq_shapes + [jax.ShapeDtypeStruct((1152, 128), F32 if last else BF16)] * parts,
        in_specs=specs,
        out_specs=[vmem] * (len(dq_shapes) + parts),
        scratch_shapes=scratch,
        compiler_params=pltpu.CompilerParams(vmem_limit_bytes=32 * 2**20),
        cost_estimate=pl.CostEstimate(
            flops=5_000_000_000 * parts, bytes_accessed=8_000_000, transcendentals=1_500_000 * parts
        ),
    )(*operands)


def chunks_kernel(
    me_ref,
    order_ref,
    lengths_ref,
    lse_ref,
    delta_ref,
    kv_ref,
    p0_ref,
    p1_ref,
    p2_ref,
    p3_ref,
    o0_ref,
    o1_ref,
    o2_ref,
    o3_ref,
    at_ref,
    prompts,
):
    head, r, c = me_ref[1], me_ref[4], me_ref[5]
    for i in range(64):
        at_ref[i] = order_ref[0, RUN * i] // RUN
    for i in range(5):
        at_ref[64 + i] = me_ref[i]
    slots = lax.broadcasted_iota(jnp.int32, (128, 32), 0)
    run = jnp.where(slots < RUN, order_ref[0, 128 * c], order_ref[0, 128 * c + RUN])
    live = run + (slots & (RUN - 1)) < lengths_ref[0]
    stats = (jnp.where(live, lse_ref[...] * LOG2E, 1e30), delta_ref[...])
    for i, ref in enumerate((p0_ref, p1_ref, p2_ref, p3_ref)):
        prompts[i] = ref[...]
    terms = []
    for j in range(2):
        rest = stats[j]
        for _ in range(3):
            term = rest.astype(BF16)
            terms.append(term)
            rest = rest - term.astype(F32)
    terms = jnp.concatenate(terms, axis=0)
    slot = lax.broadcasted_iota(jnp.int32, (768, 128), 0)
    lane = lax.broadcasted_iota(jnp.int32, (768, 128), 1)
    here = (slot & 15) == (lane >> 3)
    to_row = lax.broadcasted_iota(jnp.int32, (48, 768), 0)
    from_slot = lax.broadcasted_iota(jnp.int32, (48, 768), 1)
    gather = (to_row == (from_slot >> 4)).astype(BF16)
    from_head = lax.broadcasted_iota(jnp.int32, (32, 128), 0)
    to_head = lax.broadcasted_iota(jnp.int32, (32, 128), 1) & 7
    for s, ref in enumerate((o0_ref, o1_ref, o2_ref, o3_ref)):
        g = (head + s) & 3
        spread = dot(terms, (from_head == to_head + 8 * g).astype(BF16), NN)
        ref[pl.ds(0, 256), :] = kv_ref[g]
        ref[pl.ds(256, 32), :] = prompts[(r - g) & 3]
        ref[pl.ds(288, 48), :] = dot(gather, jnp.where(here, spread, 0.0).astype(BF16), NN).astype(BF16)


def pick(stacked, index):
    return lax.dynamic_index_in_dim(stacked, index, 0, keepdims=False)


def make_chunks(me, order, lengths, lse, delta, kv, prompts):
    vmem = pl.BlockSpec(memory_space=pltpu.VMEM)
    smem = pl.BlockSpec(memory_space=pltpu.SMEM)
    return pl.pallas_call(
        chunks_kernel,
        out_shape=[jax.ShapeDtypeStruct((336, 128), BF16)] * 4 + [jax.ShapeDtypeStruct((72,), jnp.int32)],
        in_specs=[smem] * 3 + [vmem] * 7,
        out_specs=[vmem] * 4 + [smem],
        scratch_shapes=[pltpu.VMEM((4, 32, 128), BF16)],
        compiler_params=pltpu.CompilerParams(vmem_limit_bytes=16 * 2**20),
        cost_estimate=pl.CostEstimate(flops=200_000_000, bytes_accessed=1_000_000, transcendentals=0),
    )(me, order, lengths, lse, delta, kv, *prompts)


def shards(
    queries,
    resp_keys,
    resp_values,
    prompt_keys,
    prompt_values,
    grad_out,
    attn_out,
    logsumexp,
    order,
    lengths,
):
    scale = queries.shape[3] ** (-0.5)
    r = lax.axis_index("resp")
    c = lax.axis_index("ctx")
    x, z, y, core = coords(r, c)
    head = jnp.where(core == 0, y, x)
    block = jnp.where(core == 0, x, y)

    q_four = queries[0].reshape(128, 4, 8, 128)
    g_four = grad_out[0].reshape(128, 4, 8, 128)

    def q_chunk(g):
        q = lax.dynamic_index_in_dim(q_four, g, 1, keepdims=False).reshape(1024, 128)
        do = lax.dynamic_index_in_dim(g_four, g, 1, keepdims=False).reshape(1024, 128)
        return jnp.concatenate([q, do], axis=0)

    chunks = [send(q_chunk((head + s) % 4), along_heads(s)) for s in (1, 3)]
    far_chunk = q_chunk((head + 2) % 4)

    prompt = jnp.concatenate([prompt_keys[:, 0], prompt_values[:, 0]], axis=0)
    prompts = [prompt] + [send(prompt, along_resp(s)) for s in (1, 2, 3)]
    delta = jnp.sum(grad_out[0].astype(F32) * attn_out[0].astype(F32), axis=-1)
    resp_kv = jnp.stack([resp_keys[0], resp_values[0]]).transpose(2, 0, 1, 3).reshape(4, 256, 128)
    me = jnp.stack([core, head, block, z, r, c]).astype(jnp.int32)
    *pieces, at = make_chunks(me, order, lengths, logsumexp[0], delta, resp_kv, prompts)
    pieces = [pieces[0]] + [send(pieces[s], along_heads(s)) for s in (1, 2, 3)]
    near = jnp.concatenate([piece[:288] for piece in pieces], axis=0)
    stats = jnp.concatenate([piece[288:] for piece in pieces], axis=0)
    near, far_chunk, *chunks = lax.optimization_barrier((near, far_chunk, *chunks))
    q_own, _ = lax.optimization_barrier((head, near))
    chunks = [q_chunk(q_own), chunks[0], send(far_chunk, along_heads(2)), chunks[1]]
    far = send(near, along_z())
    own = jnp.concatenate([near, far], axis=0)
    kv_blocks = {s: send(own, along_blocks(s)) for s in (1, 3)}

    dq, sent = block_grads([(0, 1)], True, False, scale, at, stats, chunks, [far], None, [])
    own, sent = lax.optimization_barrier((own, sent))
    kv_blocks[2] = send(own, along_blocks(2))
    got = [send(sent, along_z())]
    dq, near_1, far_1, near_3, far_3 = block_grads(
        [(1, 0), (1, 1), (3, 0), (3, 1)],
        False,
        False,
        scale,
        at,
        stats,
        chunks,
        [kv_blocks[1], kv_blocks[3]],
        dq,
        [],
    )
    for s, near_part, far_part in ((1, near_1, far_1), (3, near_3, far_3)):
        got += [send(near_part, along_blocks(4 - s)), send(far_part, along_both(4 - s))]
    dq, near_part, far_part = block_grads(
        [(2, 0), (2, 1)], False, False, scale, at, stats, chunks, [kv_blocks[2]], dq, got[:1]
    )
    late = [send(near_part, along_blocks(2)), send(far_part, along_both(2))]
    *dq, totals = block_grads([(0, 0)], False, True, scale, at, stats, chunks, [near], dq, got)

    *dq, late_near, late_far = lax.optimization_barrier((*dq, *late))
    late = [late_near, late_far]
    back = [dq[0]] + [send(dq[s], along_heads(4 - s)) for s in (1, 2, 3)]
    back = jnp.stack(back).reshape(4, 128, 8, 128)
    turn = (4 - head) % 4
    grad_queries = lax.dynamic_slice_in_dim(jnp.concatenate([back, back[:3]], axis=0), turn, 4, 0)
    grad_queries = grad_queries.transpose(1, 0, 2, 3).reshape(1, 128, 32, 128)

    for part in late:
        totals = totals + part.astype(F32)
    mine = totals.astype(BF16).reshape(4, 288, 128)
    rows = [mine[0]]
    for s in (1, 2, 3):
        rows.append(send(mine[s], along_heads(4 - s)))
    rows = jnp.stack(rows)
    rows = lax.dynamic_slice_in_dim(jnp.concatenate([rows, rows[:3]], axis=0), turn, 4, 0)
    grad_resp = rows[:, :256].reshape(4, 2, 128, 128).transpose(1, 2, 0, 3)
    parts = rows[:, 256:]
    mine_pair = pick(parts.reshape(2, 2, 32, 128).transpose(1, 0, 2, 3), core).astype(F32)
    theirs = pick(parts.reshape(2, 2, 32, 128).transpose(1, 0, 2, 3), 1 - core)
    mine_pair = mine_pair + send(theirs, across_cores()).astype(F32)
    theirs = send(pick(mine_pair, 1 - r // 2), across_z_hi())
    theirs, grad_queries = lax.optimization_barrier((theirs, grad_queries))
    prompt_sum = pick(mine_pair, r // 2) + theirs
    prompt_sum = prompt_sum.astype(BF16).reshape(2, 16, 128)
    return (
        grad_queries,
        grad_resp[0][None],
        grad_resp[1][None],
        prompt_sum[0][:, None],
        prompt_sum[1][:, None],
    )


def solution(mesh):
    wide = P("resp", "ctx", None, None)
    prompt = P("ctx", "resp", None)
    return jax.shard_map(
        shards,
        mesh=mesh,
        in_specs=(
            wide,
            wide,
            wide,
            prompt,
            prompt,
            wide,
            wide,
            P("resp", "ctx", None),
            P("resp", None),
            P("resp"),
        ),
        out_specs=(wide, wide, wide, prompt, prompt),
        check_vma=False,
    )
```

```python
import functools

import jax
import jax.numpy as jnp
from jax import lax
from jax.experimental import pallas as pl
from jax.experimental.pallas import tpu as pltpu
from jax.sharding import PartitionSpec as P

F32 = jnp.float32
BF16 = jnp.bfloat16
AXES = ("resp", "ctx")
LOG2E = 1.4426950408889634
RUN = 64
NT = (((1,), (1,)), ((), ()))
NN = (((1,), (0,)), ((), ()))
TN = (((0,), (0,)), ((), ()))


def coords(r, c):
    return c // 8, (c // 4) % 2, c % 4, r % 2


def device_pairs(move):
    pairs = []
    for r in range(4):
        for c in range(32):
            x, z, y, _ = coords(r, c)
            r2, x2, z2, y2 = move(r, x, z, y)
            pairs.append((r * 32 + c, (r2 % 4) * 32 + (x2 % 4) * 8 + (z2 % 2) * 4 + y2 % 4))
    return pairs


def along_heads(s):
    return device_pairs(lambda r, x, z, y: (r, x, z, y + s) if r % 2 == 0 else (r, x + s, z, y))


def along_blocks(s):
    return device_pairs(lambda r, x, z, y: (r, x + s, z, y) if r % 2 == 0 else (r, x, z, y + s))


def along_z():
    return device_pairs(lambda r, x, z, y: (r, x, z + 1, y))


def along_both(s):
    return device_pairs(lambda r, x, z, y: (r, x + s, z + 1, y) if r % 2 == 0 else (r, x, z + 1, y + s))


def along_resp(s):
    return device_pairs(lambda r, x, z, y: (r + s, x, z, y))


def across_cores():
    return device_pairs(lambda r, x, z, y: (r ^ 1, x, z, y))


def across_z_hi():
    return device_pairs(lambda r, x, z, y: (r ^ 2, x, z, y))


def send(value, pairs):
    return lax.ppermute(value, AXES, pairs)


def dot(a, b, dims):
    return lax.dot_general(a, b, dims, preferred_element_type=F32)


def grads_kernel(halves, blocks, first, last, scale, received, at_ref, stats_ref, *rest):
    parts = len(halves)
    members = 4 * parts
    rest = list(rest)
    chunk_refs = [rest.pop(0) for _ in range(4 if first else 1)]
    kv_refs = [rest.pop(0) for _ in range(blocks)]
    dq_in = None if first else rest.pop(0)
    held = [rest.pop(0) for _ in range(received)]
    dq_outs = [rest.pop(0) for _ in range(4 if last else 1)]
    outs = [rest.pop(0) for _ in range(parts)]
    chunk = rest.pop(0) if first else chunk_refs[0]
    keys, values, dkeys, dvalues, stage, meta_ref = rest[:6]
    dq = rest[6] if last else dq_outs[0]
    core, head, block, z = [at_ref[64 + i] for i in range(4)]

    def runs_of(from_b, from_h, from_z):
        c = jnp.where(core == 0, from_b * 8 + from_h, from_h * 8 + from_b) + from_z * 4
        one, two = at_ref[2 * c], at_ref[2 * c + 1]
        return jnp.minimum(one, two), jnp.where(one > two, 1, 0)

    places_in = [(part, e) for part in range(parts) for e in range(4)]
    found = [
        runs_of((block - halves[part][0]) & 3, (head - e) & 3, (z + halves[part][1]) & 1) for part, e in places_in
    ]
    for j, (early_j, swap_j) in enumerate(found):
        rank = 0
        for i, (early_i, _) in enumerate(found):
            if i != j:
                rank = rank + jnp.where(early_i < early_j, 1, 0)
        start = 1152 * places_in[j][0] + 288 * places_in[j][1]
        meta_ref[rank] = early_j
        meta_ref[16 + rank] = start + RUN * swap_j
        meta_ref[32 + rank] = start + RUN * (1 - swap_j)
    for e in range(4):
        meta_ref[48 + e], meta_ref[52 + e] = runs_of(block, (head - e) & 3, z)
    rows = 512
    prompt = 16 * members
    for i, ref in enumerate(chunk_refs if first else []):
        chunk[pl.ds(i * 2048, 2048), :] = ref[...]
    if first:
        dq[...] = jnp.zeros_like(dq)
    else:
        dq[...] = dq_in[...]
    dkeys[...] = jnp.zeros_like(dkeys)
    dvalues[...] = jnp.zeros_like(dvalues)

    def places(u):
        for late in range(2):
            at = meta_ref[16 + 16 * late + u]
            yield at, pl.ds(prompt + (late * members + u) * RUN, RUN)

    at = 0
    for ref in kv_refs:
        stage[pl.ds(at, ref.shape[0]), :] = ref[...]
        at += ref.shape[0]
    for e in range(members):
        to = pl.ds(16 * e, 16)
        keys[to, :] = stage[pl.ds(288 * e + 256, 16), :]
        values[to, :] = stage[pl.ds(288 * e + 272, 16), :]
    for u in range(members):
        for at, to in places(u):
            keys[to, :] = stage[pl.ds(pl.multiple_of(at, 16), RUN), :]
            values[to, :] = stage[pl.ds(pl.multiple_of(at + 128, 16), RUN), :]

    slope = lax.broadcasted_iota(jnp.int32, (RUN, rows), 0) - (
        lax.broadcasted_iota(jnp.int32, (RUN, rows), 1) >> 3
    )

    def one_chunk(i, _):
        base = i * 2048
        early = meta_ref[48 + i]
        early_half = meta_ref[52 + i]
        piece = stats_ref[pl.ds(pl.multiple_of(i * 48, 16), 48), :].astype(F32)

        def tile(half, spans, marks):
            q_rows = pl.ds(pl.multiple_of(base + half * rows, 16), rows)
            g_rows = pl.ds(pl.multiple_of(base + 1024 + half * rows, 16), rows)
            stats = []
            for j in range(2):
                total = piece[24 * j : 24 * j + 8] + piece[24 * j + 8 : 24 * j + 16] + piece[24 * j + 16 : 24 * j + 24]
                picked = jnp.where(half == 0, total[0:4], total[4:8])
                stats.append(jnp.concatenate([picked[k : k + 1] for k in range(4)], axis=1))
            lse2, delta = stats
            spans = [pl.ds(at, count) for at, count in spans]
            kt = jnp.concatenate([keys[span, :] for span in spans], axis=0)
            vt = jnp.concatenate([values[span, :] for span in spans], axis=0)
            q = chunk[q_rows, :]
            g = chunk[g_rows, :]
            s = dot(kt, q, NT)
            dp = dot(vt, g, NT)
            p = jnp.exp2(s * (scale * LOG2E) - lse2)
            if marks:
                cut = [p[: marks[0][0]]] if marks[0][0] else []
                for at, limit in marks:
                    cut.append(jnp.where(slope <= limit, p[at : at + RUN], 0.0))
                p = jnp.concatenate(cut, axis=0)
            ds = (p * (dp - delta)).astype(BF16)
            dv = dot(p.astype(BF16), g, NN)
            dk = dot(ds, q, NN)
            at = 0
            for span in spans:
                dvalues[span, :] += dv[at : at + span.size]
                dkeys[span, :] += dk[at : at + span.size]
                at += span.size
            acc = pl.ds(pl.multiple_of((2 * i + half) * 128, 128), 128)
            dq[acc, :] += dot(kt, ds, TN)

        def early_limit(u):
            return (early - meta_ref[u]) * RUN

        def late_limit(u):
            return (meta_ref[u] - early) * RUN

        late_half = 1 - early_half
        late_row = prompt + members * RUN
        top = members - 4
        tile(
            late_half,
            [(0, late_row), (late_row + RUN * top, 256)],
            [(late_row + RUN * u, late_limit(top + u)) for u in range(4)],
        )
        tile(early_half, [(0, prompt + 256)], [(prompt + RUN * u, early_limit(u)) for u in range(4)])
        seen = 0
        for u in range(members):
            seen = seen + jnp.where(meta_ref[u] <= early, 1, 0)
        for i_tile in range(1, parts):
            more = seen > 4 * i_tile
            low, high = 4 * i_tile, 4 * (i_tile - 1)
            tile(
                jnp.where(more, early_half, late_half),
                [(pl.multiple_of(jnp.where(more, prompt + RUN * low, late_row + RUN * high), 16), 256)],
                [(RUN * u, jnp.where(more, early_limit(low + u), late_limit(high + u))) for u in range(4)],
            )
        return 0

    lax.fori_loop(0, 4, one_chunk, 0, unroll=(4, 4, 1, 1)[parts - 1])

    if last:
        for i in range(8):
            dq_outs[i // 2][pl.ds(i % 2 * rows, rows), :] = (dq[pl.ds(i * 128, 128), :].T * scale).astype(BF16)

    wide = outs[0].dtype
    total = outs[0] if last else stage
    for e in range(members):
        at = pl.ds(16 * e, 16)
        total[pl.ds(288 * e + 256, 16), :] = (dkeys[at, :] * scale).astype(wide)
        total[pl.ds(288 * e + 272, 16), :] = dvalues[at, :].astype(wide)
    for u in range(members):
        for at, frm in places(u):
            total[pl.ds(pl.multiple_of(at, 16), RUN), :] = (dkeys[frm, :] * scale).astype(wide)
            total[pl.ds(pl.multiple_of(at + 128, 16), RUN), :] = dvalues[frm, :].astype(wide)
    if not last:
        for part in range(parts):
            outs[part][...] = stage[pl.ds(part * 1152, 1152), :]
    for ref in held if last else []:
        outs[0][...] += ref[...].astype(F32)


def block_grads(halves, first, last, scale, at, stats, chunks, kv, dq, held):
    parts = len(halves)
    members = 4 * parts
    vmem = pl.BlockSpec(memory_space=pltpu.VMEM)
    smem = pl.BlockSpec(memory_space=pltpu.SMEM)
    operands = [at, stats, *chunks, *kv] + ([] if first else [dq]) + list(held)
    specs = [smem] + [vmem] * (1 + len(chunks) + len(kv) + (0 if first else 1))
    specs += [vmem if last else pl.BlockSpec(memory_space=pl.ANY)] * len(held)
    dq_shapes = [jax.ShapeDtypeStruct((1024, 128), BF16)] * 4 if last else [jax.ShapeDtypeStruct((1024, 512), F32)]
    sorted_rows = 144 * members
    grad_shapes = [jax.ShapeDtypeStruct((1152, 128), F32 if last else BF16)] * parts
    shapes = dq_shapes + grad_shapes + ([jax.ShapeDtypeStruct((8192, 128), BF16)] if first else [])
    scratch = [
        pltpu.VMEM((sorted_rows, 128), BF16),
        pltpu.VMEM((sorted_rows, 128), BF16),
        pltpu.VMEM((sorted_rows, 128), F32),
        pltpu.VMEM((sorted_rows, 128), F32),
        pltpu.VMEM((1152 * parts, 128), BF16),
        pltpu.SMEM((64,), jnp.int32),
    ]
    if last:
        scratch.append(pltpu.VMEM((1024, 512), F32))
    return pl.pallas_call(
        functools.partial(grads_kernel, halves, len(kv), first, last, scale, len(held)),
        out_shape=shapes,
        in_specs=specs,
        out_specs=[vmem] * len(shapes),
        scratch_shapes=scratch,
        compiler_params=pltpu.CompilerParams(vmem_limit_bytes=32 * 2**20),
        cost_estimate=pl.CostEstimate(
            flops=5_000_000_000 * parts, bytes_accessed=8_000_000, transcendentals=1_500_000 * parts
        ),
    )(*operands)


def chunks_kernel(
    me_ref,
    order_ref,
    lengths_ref,
    lse_ref,
    delta_ref,
    kv_ref,
    p0_ref,
    p1_ref,
    p2_ref,
    p3_ref,
    o0_ref,
    o1_ref,
    o2_ref,
    o3_ref,
    at_ref,
    prompts,
):
    head, r, c = me_ref[1], me_ref[4], me_ref[5]
    for i in range(64):
        at_ref[i] = order_ref[0, RUN * i] // RUN
    for i in range(5):
        at_ref[64 + i] = me_ref[i]
    slots = lax.broadcasted_iota(jnp.int32, (128, 32), 0)
    run = jnp.where(slots < RUN, order_ref[0, 128 * c], order_ref[0, 128 * c + RUN])
    live = run + (slots & (RUN - 1)) < lengths_ref[0]
    stats = (jnp.where(live, lse_ref[...] * LOG2E, 1e30), delta_ref[...])
    for i, ref in enumerate((p0_ref, p1_ref, p2_ref, p3_ref)):
        prompts[i] = ref[...]
    terms = []
    for j in range(2):
        rest = stats[j]
        for _ in range(3):
            term = rest.astype(BF16)
            terms.append(term)
            rest = rest - term.astype(F32)
    terms = jnp.concatenate(terms, axis=0)
    slot = lax.broadcasted_iota(jnp.int32, (768, 128), 0)
    lane = lax.broadcasted_iota(jnp.int32, (768, 128), 1)
    here = (slot & 15) == (lane >> 3)
    to_row = lax.broadcasted_iota(jnp.int32, (48, 768), 0)
    from_slot = lax.broadcasted_iota(jnp.int32, (48, 768), 1)
    gather = (to_row == (from_slot >> 4)).astype(BF16)
    from_head = lax.broadcasted_iota(jnp.int32, (32, 128), 0)
    to_head = lax.broadcasted_iota(jnp.int32, (32, 128), 1) & 7
    for s, ref in enumerate((o0_ref, o1_ref, o2_ref, o3_ref)):
        g = (head + s) & 3
        spread = dot(terms, (from_head == to_head + 8 * g).astype(BF16), NN)
        ref[pl.ds(0, 256), :] = kv_ref[g]
        ref[pl.ds(256, 32), :] = prompts[(r - g) & 3]
        ref[pl.ds(288, 48), :] = dot(gather, jnp.where(here, spread, 0.0).astype(BF16), NN).astype(BF16)


def pick(stacked, index):
    return lax.dynamic_index_in_dim(stacked, index, 0, keepdims=False)


def make_chunks(me, order, lengths, lse, delta, kv, prompts):
    vmem = pl.BlockSpec(memory_space=pltpu.VMEM)
    smem = pl.BlockSpec(memory_space=pltpu.SMEM)
    return pl.pallas_call(
        chunks_kernel,
        out_shape=[jax.ShapeDtypeStruct((336, 128), BF16)] * 4 + [jax.ShapeDtypeStruct((72,), jnp.int32)],
        in_specs=[smem] * 3 + [vmem] * 7,
        out_specs=[vmem] * 4 + [smem],
        scratch_shapes=[pltpu.VMEM((4, 32, 128), BF16)],
        compiler_params=pltpu.CompilerParams(vmem_limit_bytes=16 * 2**20),
        cost_estimate=pl.CostEstimate(flops=200_000_000, bytes_accessed=1_000_000, transcendentals=0),
    )(me, order, lengths, lse, delta, kv, *prompts)


def shards(
    queries,
    resp_keys,
    resp_values,
    prompt_keys,
    prompt_values,
    grad_out,
    attn_out,
    logsumexp,
    order,
    lengths,
):
    scale = queries.shape[3] ** (-0.5)
    r = lax.axis_index("resp")
    c = lax.axis_index("ctx")
    x, z, y, core = coords(r, c)
    head = jnp.where(core == 0, y, x)
    block = jnp.where(core == 0, x, y)

    q_four = queries[0].reshape(128, 4, 8, 128)
    g_four = grad_out[0].reshape(128, 4, 8, 128)

    def q_chunk(g):
        q = lax.dynamic_index_in_dim(q_four, g, 1, keepdims=False).reshape(1024, 128)
        do = lax.dynamic_index_in_dim(g_four, g, 1, keepdims=False).reshape(1024, 128)
        return jnp.concatenate([q, do], axis=0)

    chunks = [send(q_chunk((head + s) % 4), along_heads(s)) for s in (1, 2)]
    last_chunk = q_chunk((head + 3) % 4)

    prompt = jnp.concatenate([prompt_keys[:, 0], prompt_values[:, 0]], axis=0)
    prompts = [prompt] + [send(prompt, along_resp(s)) for s in (1, 2, 3)]
    delta = jnp.sum(grad_out[0].astype(F32) * attn_out[0].astype(F32), axis=-1)
    resp_kv = jnp.stack([resp_keys[0], resp_values[0]]).transpose(2, 0, 1, 3).reshape(4, 256, 128)
    me = jnp.stack([core, head, block, z, r, c]).astype(jnp.int32)
    *pieces, at = make_chunks(me, order, lengths, logsumexp[0], delta, resp_kv, prompts)
    pieces = [pieces[0]] + [send(pieces[s], along_heads(s)) for s in (1, 2, 3)]
    near = jnp.concatenate([piece[:288] for piece in pieces], axis=0)
    stats = jnp.concatenate([piece[288:] for piece in pieces], axis=0)
    near, last_chunk, *chunks = lax.optimization_barrier((near, last_chunk, *chunks))
    q_own, _ = lax.optimization_barrier((head, near))
    chunks = [q_chunk(q_own), chunks[0], chunks[1], send(last_chunk, along_heads(3))]
    far = send(near, along_z())
    own = jnp.concatenate([near, far], axis=0)
    kv_blocks = {s: send(own, along_blocks(s)) for s in (1, 3)}

    dq, sent, chunk = block_grads([(0, 1)], True, False, scale, at, stats, chunks, [far], None, [])
    chunks = [chunk]
    own, sent = lax.optimization_barrier((own, sent))
    kv_blocks[2] = send(own, along_blocks(2))
    got = [send(sent, along_z())]
    dq, near_1, far_1, near_3, far_3 = block_grads(
        [(1, 0), (1, 1), (3, 0), (3, 1)],
        False,
        False,
        scale,
        at,
        stats,
        chunks,
        [kv_blocks[1], kv_blocks[3]],
        dq,
        [],
    )
    for s, near_part, far_part in ((1, near_1, far_1), (3, near_3, far_3)):
        got += [send(near_part, along_blocks(4 - s)), send(far_part, along_both(4 - s))]
    dq, near_part, far_part = block_grads(
        [(2, 0), (2, 1)], False, False, scale, at, stats, chunks, [kv_blocks[2]], dq, got[:1]
    )
    late = [send(near_part, along_blocks(2)), send(far_part, along_both(2))]
    *dq, totals = block_grads([(0, 0)], False, True, scale, at, stats, chunks, [near], dq, got)

    *dq, late_near, late_far = lax.optimization_barrier((*dq, *late))
    late = [late_near, late_far]
    back = [dq[0]] + [send(dq[s], along_heads(4 - s)) for s in (1, 2, 3)]
    back = jnp.stack(back).reshape(4, 128, 8, 128)
    turn = (4 - head) % 4
    grad_queries = lax.dynamic_slice_in_dim(jnp.concatenate([back, back[:3]], axis=0), turn, 4, 0)
    grad_queries = grad_queries.transpose(1, 0, 2, 3).reshape(1, 128, 32, 128)

    for part in late:
        totals = totals + part.astype(F32)
    mine = totals.astype(BF16).reshape(4, 288, 128)
    rows = [mine[0]]
    for s in (1, 2, 3):
        rows.append(send(mine[s], along_heads(4 - s)))
    rows = jnp.stack(rows)
    rows = lax.dynamic_slice_in_dim(jnp.concatenate([rows, rows[:3]], axis=0), turn, 4, 0)
    grad_resp = rows[:, :256].reshape(4, 2, 128, 128).transpose(1, 2, 0, 3)
    parts = rows[:, 256:]
    mine_pair = pick(parts.reshape(2, 2, 32, 128).transpose(1, 0, 2, 3), core).astype(F32)
    theirs = pick(parts.reshape(2, 2, 32, 128).transpose(1, 0, 2, 3), 1 - core)
    mine_pair = mine_pair + send(theirs, across_cores()).astype(F32)
    theirs = send(pick(mine_pair, 1 - r // 2), across_z_hi())
    theirs, grad_queries = lax.optimization_barrier((theirs, grad_queries))
    prompt_sum = pick(mine_pair, r // 2) + theirs
    prompt_sum = prompt_sum.astype(BF16).reshape(2, 16, 128)
    return (
        grad_queries,
        grad_resp[0][None],
        grad_resp[1][None],
        prompt_sum[0][:, None],
        prompt_sum[1][:, None],
    )


def solution(mesh):
    wide = P("resp", "ctx", None, None)
    prompt = P("ctx", "resp", None)
    return jax.shard_map(
        shards,
        mesh=mesh,
        in_specs=(
            wide,
            wide,
            wide,
            prompt,
            prompt,
            wide,
            wide,
            P("resp", "ctx", None),
            P("resp", None),
            P("resp"),
        ),
        out_specs=(wide, wide, wide, prompt, prompt),
        check_vma=False,
    )
```

```python
import functools

import jax
import jax.numpy as jnp
from jax import lax
from jax.experimental import pallas as pl
from jax.experimental.pallas import tpu as pltpu
from jax.sharding import PartitionSpec as P

F32 = jnp.float32
BF16 = jnp.bfloat16
AXES = ("resp", "ctx")
LOG2E = 1.4426950408889634
RUN = 64
NT = (((1,), (1,)), ((), ()))
NN = (((1,), (0,)), ((), ()))
TN = (((0,), (0,)), ((), ()))


def coords(r, c):
    return c // 8, (c // 4) % 2, c % 4, r % 2


def device_pairs(move):
    pairs = []
    for r in range(4):
        for c in range(32):
            x, z, y, _ = coords(r, c)
            r2, x2, z2, y2 = move(r, x, z, y)
            pairs.append((r * 32 + c, (r2 % 4) * 32 + (x2 % 4) * 8 + (z2 % 2) * 4 + y2 % 4))
    return pairs


def along_heads(s):
    return device_pairs(lambda r, x, z, y: (r, x, z, y + s) if r % 2 == 0 else (r, x + s, z, y))


def along_blocks(s):
    return device_pairs(lambda r, x, z, y: (r, x + s, z, y) if r % 2 == 0 else (r, x, z, y + s))


def along_z():
    return device_pairs(lambda r, x, z, y: (r, x, z + 1, y))


def along_both(s):
    return device_pairs(lambda r, x, z, y: (r, x + s, z + 1, y) if r % 2 == 0 else (r, x, z + 1, y + s))


def across_cores():
    return device_pairs(lambda r, x, z, y: (r ^ 1, x, z, y))


def across_z_hi():
    return device_pairs(lambda r, x, z, y: (r ^ 2, x, z, y))


def send(value, pairs):
    return lax.ppermute(value, AXES, pairs)


def dot(a, b, dims):
    return lax.dot_general(a, b, dims, preferred_element_type=F32)


def grads_kernel(halves, blocks, first, last, scale, received, at_ref, stats_ref, *rest):
    parts = len(halves)
    members = 4 * parts
    rest = list(rest)
    chunk_refs = [rest.pop(0) for _ in range(4 if first else 1)]
    kv_refs = [rest.pop(0) for _ in range(blocks)]
    dq_in = None if first else rest.pop(0)
    held = [rest.pop(0) for _ in range(received)]
    dq_outs = [rest.pop(0) for _ in range(4 if last else 1)]
    outs = [rest.pop(0) for _ in range(parts)]
    chunk = rest.pop(0) if first else chunk_refs[0]
    keys, values, dkeys, dvalues, stage, meta_ref = rest[:6]
    dq = rest[6] if last else dq_outs[0]
    core, head, block, z = [at_ref[64 + i] for i in range(4)]

    def runs_of(from_b, from_h, from_z):
        c = jnp.where(core == 0, from_b * 8 + from_h, from_h * 8 + from_b) + from_z * 4
        one, two = at_ref[2 * c], at_ref[2 * c + 1]
        return jnp.minimum(one, two), jnp.where(one > two, 1, 0)

    places_in = [(part, e) for part in range(parts) for e in range(4)]
    found = [
        runs_of((block - halves[part][0]) & 3, (head - e) & 3, (z + halves[part][1]) & 1) for part, e in places_in
    ]
    for j, (early_j, swap_j) in enumerate(found):
        rank = 0
        for i, (early_i, _) in enumerate(found):
            if i != j:
                rank = rank + jnp.where(early_i < early_j, 1, 0)
        start = 1152 * places_in[j][0] + 288 * places_in[j][1]
        meta_ref[rank] = early_j
        meta_ref[16 + rank] = start + RUN * swap_j
        meta_ref[32 + rank] = start + RUN * (1 - swap_j)
    for e in range(4):
        meta_ref[48 + e], meta_ref[52 + e] = runs_of(block, (head - e) & 3, z)
    rows = 512
    prompt = 16 * members
    for i, ref in enumerate(chunk_refs if first else []):
        chunk[pl.ds(i * 2048, 2048), :] = ref[...]
    if first:
        dq[...] = jnp.zeros_like(dq)
    else:
        dq[...] = dq_in[...]
    dkeys[...] = jnp.zeros_like(dkeys)
    dvalues[...] = jnp.zeros_like(dvalues)

    def places(u):
        for late in range(2):
            at = meta_ref[16 + 16 * late + u]
            yield at, pl.ds(prompt + (late * members + u) * RUN, RUN)

    at = 0
    for ref in kv_refs:
        stage[pl.ds(at, ref.shape[0]), :] = ref[...]
        at += ref.shape[0]
    for e in range(members):
        to = pl.ds(16 * e, 16)
        keys[to, :] = stage[pl.ds(288 * e + 256, 16), :]
        values[to, :] = stage[pl.ds(288 * e + 272, 16), :]
    for u in range(members):
        for at, to in places(u):
            keys[to, :] = stage[pl.ds(pl.multiple_of(at, 16), RUN), :]
            values[to, :] = stage[pl.ds(pl.multiple_of(at + 128, 16), RUN), :]

    slope = lax.broadcasted_iota(jnp.int32, (RUN, rows), 0) - (
        lax.broadcasted_iota(jnp.int32, (RUN, rows), 1) >> 3
    )

    def one_chunk(i, _):
        base = i * 2048
        early = meta_ref[48 + i]
        early_half = meta_ref[52 + i]
        piece = stats_ref[pl.ds(pl.multiple_of(i * 48, 16), 48), :].astype(F32)

        def tile(half, spans, marks):
            q_rows = pl.ds(pl.multiple_of(base + half * rows, 16), rows)
            g_rows = pl.ds(pl.multiple_of(base + 1024 + half * rows, 16), rows)
            stats = []
            for j in range(2):
                total = piece[24 * j : 24 * j + 8] + piece[24 * j + 8 : 24 * j + 16] + piece[24 * j + 16 : 24 * j + 24]
                picked = jnp.where(half == 0, total[0:4], total[4:8])
                stats.append(jnp.concatenate([picked[k : k + 1] for k in range(4)], axis=1))
            lse2, delta = stats
            spans = [pl.ds(at, count) for at, count in spans]
            kt = jnp.concatenate([keys[span, :] for span in spans], axis=0)
            vt = jnp.concatenate([values[span, :] for span in spans], axis=0)
            q = chunk[q_rows, :]
            g = chunk[g_rows, :]
            s = dot(kt, q, NT)
            dp = dot(vt, g, NT)
            p = jnp.exp2(s * (scale * LOG2E) - lse2)
            if marks:
                cut = [p[: marks[0][0]]] if marks[0][0] else []
                for at, limit in marks:
                    cut.append(jnp.where(slope <= limit, p[at : at + RUN], 0.0))
                p = jnp.concatenate(cut, axis=0)
            ds = (p * (dp - delta)).astype(BF16)
            dv = dot(p.astype(BF16), g, NN)
            dk = dot(ds, q, NN)
            at = 0
            for span in spans:
                dvalues[span, :] += dv[at : at + span.size]
                dkeys[span, :] += dk[at : at + span.size]
                at += span.size
            acc = pl.ds(pl.multiple_of((2 * i + half) * 128, 128), 128)
            dq[acc, :] += dot(kt, ds, TN)

        def early_limit(u):
            return (early - meta_ref[u]) * RUN

        def late_limit(u):
            return (meta_ref[u] - early) * RUN

        late_half = 1 - early_half
        late_row = prompt + members * RUN
        top = members - 4
        tile(
            late_half,
            [(0, late_row), (late_row + RUN * top, 256)],
            [(late_row + RUN * u, late_limit(top + u)) for u in range(4)],
        )
        tile(early_half, [(0, prompt + 256)], [(prompt + RUN * u, early_limit(u)) for u in range(4)])
        seen = 0
        for u in range(members):
            seen = seen + jnp.where(meta_ref[u] <= early, 1, 0)
        for i_tile in range(1, parts):
            more = seen > 4 * i_tile
            low, high = 4 * i_tile, 4 * (i_tile - 1)
            tile(
                jnp.where(more, early_half, late_half),
                [(pl.multiple_of(jnp.where(more, prompt + RUN * low, late_row + RUN * high), 16), 256)],
                [(RUN * u, jnp.where(more, early_limit(low + u), late_limit(high + u))) for u in range(4)],
            )
        return 0

    lax.fori_loop(0, 4, one_chunk, 0, unroll=(4, 4, 1, 1)[parts - 1])

    if last:
        for i in range(8):
            dq_outs[i // 2][pl.ds(i % 2 * rows, rows), :] = (dq[pl.ds(i * 128, 128), :].T * scale).astype(BF16)

    wide = outs[0].dtype
    total = outs[0] if last else stage
    for e in range(members):
        at = pl.ds(16 * e, 16)
        total[pl.ds(288 * e + 256, 16), :] = (dkeys[at, :] * scale).astype(wide)
        total[pl.ds(288 * e + 272, 16), :] = dvalues[at, :].astype(wide)
    for u in range(members):
        for at, frm in places(u):
            total[pl.ds(pl.multiple_of(at, 16), RUN), :] = (dkeys[frm, :] * scale).astype(wide)
            total[pl.ds(pl.multiple_of(at + 128, 16), RUN), :] = dvalues[frm, :].astype(wide)
    if not last:
        for part in range(parts):
            outs[part][...] = stage[pl.ds(part * 1152, 1152), :]
    for ref in held if last else []:
        outs[0][...] += ref[...].astype(F32)


def block_grads(halves, first, last, scale, at, stats, chunks, kv, dq, held):
    parts = len(halves)
    members = 4 * parts
    vmem = pl.BlockSpec(memory_space=pltpu.VMEM)
    smem = pl.BlockSpec(memory_space=pltpu.SMEM)
    operands = [at, stats, *chunks, *kv] + ([] if first else [dq]) + list(held)
    specs = [smem] + [vmem] * (1 + len(chunks) + len(kv) + (0 if first else 1))
    specs += [vmem if last else pl.BlockSpec(memory_space=pl.ANY)] * len(held)
    dq_shapes = [jax.ShapeDtypeStruct((1024, 128), BF16)] * 4 if last else [jax.ShapeDtypeStruct((1024, 512), F32)]
    sorted_rows = 144 * members
    grad_shapes = [jax.ShapeDtypeStruct((1152, 128), F32 if last else BF16)] * parts
    shapes = dq_shapes + grad_shapes + ([jax.ShapeDtypeStruct((8192, 128), BF16)] if first else [])
    scratch = [
        pltpu.VMEM((sorted_rows, 128), BF16),
        pltpu.VMEM((sorted_rows, 128), BF16),
        pltpu.VMEM((sorted_rows, 128), F32),
        pltpu.VMEM((sorted_rows, 128), F32),
        pltpu.VMEM((1152 * parts, 128), BF16),
        pltpu.SMEM((64,), jnp.int32),
    ]
    if last:
        scratch.append(pltpu.VMEM((1024, 512), F32))
    return pl.pallas_call(
        functools.partial(grads_kernel, halves, len(kv), first, last, scale, len(held)),
        out_shape=shapes,
        in_specs=specs,
        out_specs=[vmem] * len(shapes),
        scratch_shapes=scratch,
        compiler_params=pltpu.CompilerParams(vmem_limit_bytes=32 * 2**20),
        cost_estimate=pl.CostEstimate(
            flops=5_000_000_000 * parts, bytes_accessed=8_000_000, transcendentals=1_500_000 * parts
        ),
    )(*operands)


def chunks_kernel(
    me_ref,
    order_ref,
    lengths_ref,
    lse_ref,
    delta_ref,
    kv_ref,
    near_ref,
    far_ref,
    o0_ref,
    o1_ref,
    o2_ref,
    o3_ref,
    at_ref,
    prompts,
):
    head, r, c = me_ref[1], me_ref[4], me_ref[5]
    for i in range(64):
        at_ref[i] = order_ref[0, RUN * i] // RUN
    for i in range(5):
        at_ref[64 + i] = me_ref[i]
    slots = lax.broadcasted_iota(jnp.int32, (128, 32), 0)
    run = jnp.where(slots < RUN, order_ref[0, 128 * c], order_ref[0, 128 * c + RUN])
    live = run + (slots & (RUN - 1)) < lengths_ref[0]
    stats = (jnp.where(live, lse_ref[...] * LOG2E, 1e30), delta_ref[...])
    for i, ref in enumerate((near_ref, far_ref)):
        prompts[2 * i] = ref[pl.ds(0, 32), :]
        prompts[2 * i + 1] = ref[pl.ds(32, 32), :]
    terms = []
    for j in range(2):
        rest = stats[j]
        for _ in range(3):
            term = rest.astype(BF16)
            terms.append(term)
            rest = rest - term.astype(F32)
    terms = jnp.concatenate(terms, axis=0)
    slot = lax.broadcasted_iota(jnp.int32, (768, 128), 0)
    lane = lax.broadcasted_iota(jnp.int32, (768, 128), 1)
    here = (slot & 15) == (lane >> 3)
    to_row = lax.broadcasted_iota(jnp.int32, (48, 768), 0)
    from_slot = lax.broadcasted_iota(jnp.int32, (48, 768), 1)
    gather = (to_row == (from_slot >> 4)).astype(BF16)
    from_head = lax.broadcasted_iota(jnp.int32, (32, 128), 0)
    to_head = lax.broadcasted_iota(jnp.int32, (32, 128), 1) & 7
    for s, ref in enumerate((o0_ref, o1_ref, o2_ref, o3_ref)):
        g = (head + s) & 3
        spread = dot(terms, (from_head == to_head + 8 * g).astype(BF16), NN)
        ref[pl.ds(0, 256), :] = kv_ref[g]
        ref[pl.ds(256, 32), :] = prompts[r ^ g]
        ref[pl.ds(288, 48), :] = dot(gather, jnp.where(here, spread, 0.0).astype(BF16), NN).astype(BF16)


def pick(stacked, index):
    return lax.dynamic_index_in_dim(stacked, index, 0, keepdims=False)


def make_chunks(me, order, lengths, lse, delta, kv, prompts):
    vmem = pl.BlockSpec(memory_space=pltpu.VMEM)
    smem = pl.BlockSpec(memory_space=pltpu.SMEM)
    return pl.pallas_call(
        chunks_kernel,
        out_shape=[jax.ShapeDtypeStruct((336, 128), BF16)] * 4 + [jax.ShapeDtypeStruct((72,), jnp.int32)],
        in_specs=[smem] * 3 + [vmem] * 5,
        out_specs=[vmem] * 4 + [smem],
        scratch_shapes=[pltpu.VMEM((4, 32, 128), BF16)],
        compiler_params=pltpu.CompilerParams(vmem_limit_bytes=16 * 2**20),
        cost_estimate=pl.CostEstimate(flops=200_000_000, bytes_accessed=1_000_000, transcendentals=0),
    )(me, order, lengths, lse, delta, kv, *prompts)


def shards(
    queries,
    resp_keys,
    resp_values,
    prompt_keys,
    prompt_values,
    grad_out,
    attn_out,
    logsumexp,
    order,
    lengths,
):
    scale = queries.shape[3] ** (-0.5)
    r = lax.axis_index("resp")
    c = lax.axis_index("ctx")
    x, z, y, core = coords(r, c)
    head = jnp.where(core == 0, y, x)
    block = jnp.where(core == 0, x, y)

    q_four = queries[0].reshape(128, 4, 8, 128)
    g_four = grad_out[0].reshape(128, 4, 8, 128)

    def q_chunk(g):
        q = lax.dynamic_index_in_dim(q_four, g, 1, keepdims=False).reshape(1024, 128)
        do = lax.dynamic_index_in_dim(g_four, g, 1, keepdims=False).reshape(1024, 128)
        return jnp.concatenate([q, do], axis=0)

    chunks = [send(q_chunk((head + s) % 4), along_heads(s)) for s in (1, 2)]
    last_chunk = q_chunk((head + 3) % 4)

    prompt = jnp.concatenate([prompt_keys[:, 0], prompt_values[:, 0]], axis=0)
    prompt = jnp.concatenate([prompt, send(prompt, across_cores())], axis=0)
    prompts = [prompt, send(prompt, across_z_hi())]
    delta = jnp.sum(grad_out[0].astype(F32) * attn_out[0].astype(F32), axis=-1)
    resp_kv = jnp.stack([resp_keys[0], resp_values[0]]).transpose(2, 0, 1, 3).reshape(4, 256, 128)
    me = jnp.stack([core, head, block, z, r, c]).astype(jnp.int32)
    *pieces, at = make_chunks(me, order, lengths, logsumexp[0], delta, resp_kv, prompts)
    pieces = [pieces[0]] + [send(pieces[s], along_heads(s)) for s in (1, 2, 3)]
    near = jnp.concatenate([piece[:288] for piece in pieces], axis=0)
    stats = jnp.concatenate([piece[288:] for piece in pieces], axis=0)
    near, last_chunk, *chunks = lax.optimization_barrier((near, last_chunk, *chunks))
    q_own, _ = lax.optimization_barrier((head, near))
    chunks = [q_chunk(q_own), chunks[0], chunks[1], send(last_chunk, along_heads(3))]
    far = send(near, along_z())
    own = jnp.concatenate([near, far], axis=0)
    kv_blocks = {s: send(own, along_blocks(s)) for s in (1, 3)}

    dq, sent, chunk = block_grads([(0, 1)], True, False, scale, at, stats, chunks, [far], None, [])
    chunks = [chunk]
    own, sent = lax.optimization_barrier((own, sent))
    kv_blocks[2] = send(own, along_blocks(2))
    got = [send(sent, along_z())]
    dq, near_1, far_1, near_3, far_3 = block_grads(
        [(1, 0), (1, 1), (3, 0), (3, 1)],
        False,
        False,
        scale,
        at,
        stats,
        chunks,
        [kv_blocks[1], kv_blocks[3]],
        dq,
        [],
    )
    for s, near_part, far_part in ((1, near_1, far_1), (3, near_3, far_3)):
        got += [send(near_part, along_blocks(4 - s)), send(far_part, along_both(4 - s))]
    dq, near_part, far_part = block_grads(
        [(2, 0), (2, 1)], False, False, scale, at, stats, chunks, [kv_blocks[2]], dq, got[:1]
    )
    late = [send(near_part, along_blocks(2)), send(far_part, along_both(2))]
    *dq, totals = block_grads([(0, 0)], False, True, scale, at, stats, chunks, [near], dq, got)

    *dq, late_near, late_far = lax.optimization_barrier((*dq, *late))
    late = [late_near, late_far]
    back = [dq[0]] + [send(dq[s], along_heads(4 - s)) for s in (1, 2, 3)]
    back = jnp.stack(back).reshape(4, 128, 8, 128)
    turn = (4 - head) % 4
    grad_queries = lax.dynamic_slice_in_dim(jnp.concatenate([back, back[:3]], axis=0), turn, 4, 0)
    grad_queries = grad_queries.transpose(1, 0, 2, 3).reshape(1, 128, 32, 128)

    for part in late:
        totals = totals + part.astype(F32)
    mine = totals.astype(BF16).reshape(4, 288, 128)
    rows = [mine[0]]
    for s in (1, 2, 3):
        rows.append(send(mine[s], along_heads(4 - s)))
    rows = jnp.stack(rows)
    rows = lax.dynamic_slice_in_dim(jnp.concatenate([rows, rows[:3]], axis=0), turn, 4, 0)
    grad_resp = rows[:, :256].reshape(4, 2, 128, 128).transpose(1, 2, 0, 3)
    parts = rows[:, 256:]
    mine_pair = pick(parts.reshape(2, 2, 32, 128).transpose(1, 0, 2, 3), core).astype(F32)
    theirs = pick(parts.reshape(2, 2, 32, 128).transpose(1, 0, 2, 3), 1 - core)
    mine_pair = mine_pair + send(theirs, across_cores()).astype(F32)
    theirs = send(pick(mine_pair, 1 - r // 2), across_z_hi())
    theirs, grad_queries = lax.optimization_barrier((theirs, grad_queries))
    prompt_sum = pick(mine_pair, r // 2) + theirs
    prompt_sum = prompt_sum.astype(BF16).reshape(2, 16, 128)
    return (
        grad_queries,
        grad_resp[0][None],
        grad_resp[1][None],
        prompt_sum[0][:, None],
        prompt_sum[1][:, None],
    )


def solution(mesh):
    wide = P("resp", "ctx", None, None)
    prompt = P("ctx", "resp", None)
    return jax.shard_map(
        shards,
        mesh=mesh,
        in_specs=(
            wide,
            wide,
            wide,
            prompt,
            prompt,
            wide,
            wide,
            P("resp", "ctx", None),
            P("resp", None),
            P("resp"),
        ),
        out_specs=(wide, wide, wide, prompt, prompt),
        check_vma=False,
    )
```
